256 devices in a mesh: clips: 16 (over x_hi, y, core), tm: 16 (over z, x_lo).
Axes of the slice: x: 4 (x_hi: 2, x_lo: 2; x = x_hi * 2 + x_lo), y: 4, z: 8, core: 2. Of those that a mesh axis runs over, the one named last changes fastest.
Arguments:
- video: bfloat16 [16, 256, 8, 8, 256], P('clips', 'tm'), may hold values from -6 to 6
- cotangent: bfloat16 [16, 128, 4, 4, 1024], P('clips', 'tm'), may hold values from -0.01171875 to 0.01171875
- gains: float32 [2, 256], replicated, may hold values from 0.5 to 2
- spatial_weights: bfloat16 [2, 3, 3, 256, 256], replicated, may hold values from -0.125 to 0.125
- time_weights: bfloat16 [2, 3, 256, 256], replicated, may hold values from -0.21875 to 0.21875
- reduce_kernel_weights: bfloat16 [3, 256, 256], replicated, may hold values from -0.21875 to 0.21875
Outputs:
- encoded: bfloat16 [16, 128, 4, 4, 1024], P('clips', 'tm')
- grad_spatial: float32 [2, 3, 3, 256, 256], replicated
- grad_time: float32 [2, 3, 256, 256], replicated
- grad_down: float32 [3, 256, 256], replicated
- grad_gains: float32 [2, 256], replicated
The draws below stay inside these ranges and needn't reach their ends.
All inputs are finite; a program needn't handle non-finite values.
Results may differ from the reference program's by a relative error of at most 0.017.
Values may be sent and summed in bfloat16 or wider, within the bound.
No kernel may reach another device: no remote copies, remote signals or barrier semaphores. Data moves between devices by JAX's collectives and lax.ppermute only.
A program may use at most 128 MiB of HBM per device.

```python
import math
import jax
import jax.numpy as jnp
from jax import lax

C = 256
SIDE = 8
BLOCKS = 2
CLIP_DEV = 1
FR_DEV = 16
CLIPS = 16
FRAMES = 256
N_CLIPS = 16
N_TM = 16


def block_scale(own_key, dims, cuts, smallest, largest):
    def one(dim, blocks):
        heights = jax.random.uniform(jax.random.fold_in(jax.random.fold_in(own_key, 6), dim), (blocks,), jnp.float32, smallest / len(cuts), largest / len(cuts))
        return jnp.repeat(jnp.exp(heights), dims[dim] // blocks).reshape((-1,) + (1,) * (len(dims) - dim - 1))

    factor_of = one(*cuts[0])
    for cut in cuts[1:]:
        factor_of = factor_of * one(*cut)
    return factor_of


def scatter_about(key, extent, width, bound, shards=(), dtype=jnp.bfloat16):
    array = width * jax.random.normal(key, extent, jnp.float32)
    if shards:
        array = array * block_scale(key, extent, shards, -0.22, 0.18)
    return jnp.clip(array, -bound, bound).astype(dtype)


def setup_inputs(seed: int = 0) -> dict:
    key_of = jax.random.split(jax.random.key(seed), 7)
    video = scatter_about(key_of[0], (CLIPS, FRAMES, SIDE, SIDE, C), 1.0, 6.0, ((0, 16), (1, 16)))
    cotangent = scatter_about(key_of[1], (CLIPS, FR_DEV * N_TM // 2, SIDE // 2, SIDE // 2, 4 * C), ((CLIP_DEV * N_CLIPS * FR_DEV * N_TM * SIDE * SIDE) ** -0.5), 0.01171875, ((0, 16), (1, 16)))
    gains = jnp.clip(jnp.exp(jax.random.uniform(key_of[2], (BLOCKS, C), jnp.float32, math.log(0.5), math.log(2.0))), 0.5, 2.0)
    spatial_weights = scatter_about(key_of[3], (BLOCKS, 3, 3, C, C), (9 * C) ** -0.5, 0.125)
    time_weights = scatter_about(key_of[4], (BLOCKS, 3, C, C), (3 * C) ** -0.5, 0.21875)
    reduce_kernel_weights = scatter_about(key_of[5], (3, C, C), (3 * C) ** -0.5, 0.21875)
    return dict(video=video, cotangent=cotangent, gains=gains, spatial_weights=spatial_weights, time_weights=time_weights, reduce_kernel_weights=reduce_kernel_weights)


EPSILON = 1e-06

def normed(stream, gain):
    scale_inv = lax.rsqrt(lax.optimization_barrier(jnp.mean(stream * stream, axis=-1, keepdims=True)) + EPSILON)
    return stream * scale_inv * gain

def pad_space(values):
    return jnp.pad(values, ((0, 0), (0, 0), (1, 1), (1, 1), (0, 0)))

def spatial(normed_in, weight_tensors):
    side_len = normed_in.shape[2]
    padded = pad_space(normed_in)
    summed = jnp.zeros(normed_in.shape[:-1] + (weight_tensors.shape[-1],), jnp.float32)
    for row_shift in range(3):
        for col_shift in range(3):
            window = padded[:, :, row_shift:row_shift + side_len, col_shift:col_shift + side_len]
            summed = summed + jnp.dot(window, weight_tensors[row_shift, col_shift], preferred_element_type=jnp.float32)
    return summed

def outer_sum(left, right):
    return lax.dot_general(left.reshape(-1, left.shape[-1]), right.reshape(-1, right.shape[-1]), (((0,), (0,)), ((), ())), preferred_element_type=jnp.float32)

def spatial_grad(normed_in, grad_pre, weight_tensors):
    side_len = normed_in.shape[2]
    padded_in = pad_space(normed_in)
    padded_grad = pad_space(grad_pre)
    grad_norm = jnp.zeros(normed_in.shape, jnp.float32)
    rows_out = []
    for row_shift in range(3):
        cols_out = []
        for col_shift in range(3):
            window = padded_in[:, :, row_shift:row_shift + side_len, col_shift:col_shift + side_len]
            cols_out.append(outer_sum(window, grad_pre))
            back = padded_grad[:, :, 2 - row_shift:2 - row_shift + side_len, 2 - col_shift:2 - col_shift + side_len]
            grad_norm = grad_norm + jnp.dot(back, weight_tensors[row_shift, col_shift].T, preferred_element_type=jnp.float32)
        rows_out.append(jnp.stack(cols_out))
    return (jnp.stack(rows_out), grad_norm)

def silu_slope(conv_out):
    logistic = jax.nn.sigmoid(conv_out)
    return logistic * (1.0 + conv_out * (1.0 - logistic))

def norm_back(stream, gain, grad_norm):
    _, pullback = jax.vjp(normed, stream, gain)
    return pullback(grad_norm)

def section_in(stream, gain, weight_tensors):
    normed_in = normed(stream, gain).astype(jnp.bfloat16)
    conv_out = spatial(normed_in, weight_tensors)
    activated = jax.nn.silu(conv_out).astype(jnp.bfloat16)
    return (normed_in, conv_out, activated)

def temporal(with_edge, weight_tensors):
    frame_count = with_edge.shape[1] - 2
    summed = jnp.zeros((with_edge.shape[0], frame_count) + with_edge.shape[2:-1] + (weight_tensors.shape[-1],), jnp.float32)
    for kernel_tap in range(3):
        summed = summed + jnp.dot(with_edge[:, 2 - kernel_tap:2 - kernel_tap + frame_count], weight_tensors[kernel_tap], preferred_element_type=jnp.float32)
    return summed

def time_grad(with_edge, grad_bf, later_edge, weight_tensors):
    frame_count = grad_bf.shape[1]
    grad_weights = jnp.stack([outer_sum(with_edge[:, 2 - kernel_tap:2 - kernel_tap + frame_count], grad_bf) for kernel_tap in range(3)])
    padded_later = jnp.concatenate([grad_bf, later_edge], axis=1)
    grad_act = jnp.zeros(grad_bf.shape, jnp.float32)
    for kernel_tap in range(3):
        grad_act = grad_act + jnp.dot(padded_later[:, kernel_tap:kernel_tap + frame_count], weight_tensors[kernel_tap].T, preferred_element_type=jnp.float32)
    return (grad_weights, grad_act)

def regroup(values):
    clips, halves, side_len, _, channels = values.shape
    split = values.reshape(clips, halves, side_len // 2, 2, side_len // 2, 2, channels)
    return split.transpose(0, 1, 2, 4, 3, 5, 6).reshape(clips, halves, side_len // 2, side_len // 2, 4 * channels)

def ungroup(values):
    clips, halves, half_side, _, wide_channels = values.shape
    channels = wide_channels // 4
    split = values.reshape(clips, halves, half_side, half_side, 2, 2, channels)
    return split.transpose(0, 1, 2, 4, 3, 5, 6).reshape(clips, halves, 2 * half_side, 2 * half_side, channels)

def temporal_reduce(lowered_program, preceding_odd_frame, weight_tensors):
    clips, frame_count, side_len, _, channels = lowered_program.shape
    frame_pairs = lowered_program.reshape(clips, frame_count // 2, 2, side_len, side_len, channels)
    even_frames = frame_pairs[:, :, 0]
    odd_frames = frame_pairs[:, :, 1]
    prev_frames = jnp.concatenate([preceding_odd_frame, odd_frames[:, :-1]], axis=1)
    encoded_result = jnp.dot(odd_frames, weight_tensors[0], preferred_element_type=jnp.float32)
    encoded_result = encoded_result + jnp.dot(even_frames, weight_tensors[1], preferred_element_type=jnp.float32)
    encoded_result = encoded_result + jnp.dot(prev_frames, weight_tensors[2], preferred_element_type=jnp.float32)
    return (encoded_result, (odd_frames, even_frames, prev_frames))

def down_grad(frame_collections, cot_frames, cot_after, weight_tensors):
    odd_frames, even_frames, prev_frames = frame_collections
    grad_weights = jnp.stack([outer_sum(odd_frames, cot_frames), outer_sum(even_frames, cot_frames), outer_sum(prev_frames, cot_frames)])
    cot_next = jnp.concatenate([cot_frames[:, 1:], cot_after], axis=1)
    grad_odd = jnp.dot(cot_frames, weight_tensors[0].T, preferred_element_type=jnp.float32)
    grad_odd = grad_odd + jnp.dot(cot_next, weight_tensors[2].T, preferred_element_type=jnp.float32)
    grad_even = jnp.dot(cot_frames, weight_tensors[1].T, preferred_element_type=jnp.float32)
    clips, halves, side_len, _, channels = grad_odd.shape
    upstream = jnp.stack([grad_even, grad_odd], axis=2).reshape(clips, 2 * halves, side_len, side_len, channels)
    return (grad_weights, upstream)

def reference(video, cotangent, gains, spatial_weights, time_weights, reduce_kernel_weights):
    block_count = spatial_weights.shape[0]

    def one_clip(running, clip_item):
        clip_video, clip_cot = clip_item
        stream = clip_video[None].astype(jnp.float32)
        stored = []
        for which_block in range(block_count):
            normed_in, conv_out, activated = section_in(stream, gains[which_block], spatial_weights[which_block])
            with_edge = jnp.concatenate([jnp.zeros_like(activated[:, :2]), activated], axis=1)
            stored.append((stream, normed_in, conv_out, with_edge))
            stream = stream + temporal(with_edge, time_weights[which_block])
        lowered_program = stream.astype(jnp.bfloat16)
        encoded_result, frame_collections = temporal_reduce(lowered_program, jnp.zeros_like(lowered_program[:, :1]), reduce_kernel_weights)
        encoded = regroup(encoded_result.astype(jnp.bfloat16))
        cot_frames = ungroup(clip_cot[None])
        grad_dn, upstream = down_grad(frame_collections, cot_frames, jnp.zeros_like(cot_frames[:, :1]), reduce_kernel_weights)
        list_sp, list_tm, list_gn = ([], [], [])
        for which_block in reversed(range(block_count)):
            stream_in, normed_in, conv_out, with_edge = stored[which_block]
            grad_bf = upstream.astype(jnp.bfloat16)
            grad_tm, grad_act = time_grad(with_edge, grad_bf, jnp.zeros_like(grad_bf[:, :2]), time_weights[which_block])
            grad_pre = (grad_act * silu_slope(conv_out)).astype(jnp.bfloat16)
            grad_sp, grad_norm = spatial_grad(normed_in, grad_pre, spatial_weights[which_block])
            grad_stream, grad_gain = norm_back(stream_in, gains[which_block], grad_norm)
            upstream = upstream + grad_stream
            list_sp.append(grad_sp)
            list_tm.append(grad_tm)
            list_gn.append(grad_gain)
        added = (jnp.stack(list_sp[::-1]), jnp.stack(list_tm[::-1]), grad_dn, jnp.stack(list_gn[::-1]))
        running = tuple((prior + extra for prior, extra in zip(running, added)))
        return (running, encoded[0])
    start = (jnp.zeros(spatial_weights.shape, jnp.float32), jnp.zeros(time_weights.shape, jnp.float32), jnp.zeros(reduce_kernel_weights.shape, jnp.float32), jnp.zeros(gains.shape, jnp.float32))
    finals, encoded = lax.scan(one_clip, start, (video, cotangent))
    return (encoded, finals[0], finals[1], finals[2], finals[3])
```

```python
import jax
import jax.numpy as jnp
from jax import lax
from jax.experimental import pallas as pl
from jax.experimental.pallas import tpu as pltpu
from jax.sharding import Mesh, PartitionSpec as P

EPSILON = 1e-06
F32 = jnp.float32
BF16 = jnp.bfloat16
C = 256
PIX = 64
FR = 16
MATS = 27
ROWS = MATS * C
CHUNK = 448
FLAT = 16 * CHUNK
EVERY = ("xh", "y", "core", "z", "xl")
PLANE = ("xh", "xl", "y")


def dot(left, right):
    return jnp.dot(left, right, preferred_element_type=F32)


def dot_nt(left, right):
    return lax.dot_general(left, right, (((1,), (1,)), ((), ())), preferred_element_type=F32)


def dot_tn(left, right):
    return lax.dot_general(left, right, (((0,), (0,)), ((), ())), preferred_element_type=F32)


def frames(first, count):
    return pl.ds(first * PIX, count * PIX)


def one_frame(index):
    return pl.ds(pl.multiple_of(index * PIX, PIX), PIX)


def write_windows(value, im_ref, rows, sign):
    grid = value.reshape(8, 8, C)
    column = lax.broadcasted_iota(jnp.int32, (8, 8, C), 1)
    blank = jnp.zeros((1, 8, C), F32)
    for j in range(3):
        dx = sign * (j - 1)
        if dx == 0:
            moved = grid
        elif dx == 1:
            moved = jnp.where(column == 7, 0.0, pltpu.roll(grid, 7, 1))
        else:
            moved = jnp.where(column == 0, 0.0, pltpu.roll(grid, 1, 1))
        for i in range(3):
            dy = sign * (i - 1)
            if dy == 0:
                placed = moved
            elif dy == 1:
                placed = jnp.concatenate([moved[1:], blank], axis=0)
            else:
                placed = jnp.concatenate([blank, moved[:-1]], axis=0)
            tap = 3 * i + j
            im_ref[rows, tap * C : (tap + 1) * C] = placed.reshape(PIX, C).astype(BF16)


def place_matrix(groups):
    size = groups * 8
    dest = lax.broadcasted_iota(jnp.int32, (size, size), 0)
    src = lax.broadcasted_iota(jnp.int32, (size, size), 1)
    want = (dest & 1) * (groups * 4) + (dest >> 3) * 4 + ((dest >> 1) & 3)
    return jnp.where(src == want, 1.0, 0.0).astype(BF16)


def ungroup(cot_ref, groups, one_hot):
    halves = []
    for i in range(2):
        both = jnp.concatenate(
            [cot_ref[:, (2 * i + j) * C : (2 * i + j + 1) * C] for j in range(2)], axis=0
        )
        halves.append(dot(one_hot, both).reshape(groups, 8, C))
    return jnp.concatenate(halves, axis=1).reshape(groups * 16, C).astype(BF16)


def model_kernel(
    video_ref,
    before_ref,
    after_ref,
    cot_ref,
    cot_after_ref,
    gains_ref,
    sw_ref,
    tw_ref,
    rw_ref,
    enc_ref,
    grad_ref,
    s1,
    s2,
    im,
    n_refs,
    a1,
    a2,
    slope1,
    slope2,
    low,
    cotf,
    up,
    g2,
    g1,
    ga,
    gn,
    wcat,
):
    s1[frames(0, 6), :] = before_ref[...].astype(F32)
    s1[frames(6, 16), :] = video_ref[...].astype(F32)
    s1[frames(22, 2), :] = after_ref[...].astype(F32)

    def put(matrix, value):
        rows = pl.ds(matrix * C, C)
        for half in range(2):
            grad_ref[half, rows, :] = value[:, half * 128 : (half + 1) * 128].astype(BF16)

    def norm_windows(src, count, own, gain, n_ref):
        def body(index, _):
            rows = one_frame(index)
            value = src[rows, :]
            inv = lax.rsqrt(jnp.mean(value * value, axis=-1, keepdims=True) + EPSILON)
            value = value * inv * gain
            write_windows(value, im, rows, 1)

            @pl.when((index >= own) & (index < own + FR))
            def _():
                n_ref[one_frame(index - own), :] = value.astype(BF16)

            return 0

        lax.fori_loop(0, count, body, 0)

    def activate(block, pieces, act, slope):
        weights = sw_ref[block].reshape(9 * C, C)
        for first, size in pieces:
            rows = pl.ds(first, size)
            conv = dot(im[rows, :], weights)
            logistic = jax.nn.sigmoid(conv)
            act[rows, :] = (conv * logistic).astype(BF16)
            slope[rows, :] = logistic * (1.0 + conv * (1.0 - logistic))

    def temporal(act, first, count, block):
        with_edge = jnp.concatenate([act[frames(first - k, count), :] for k in range(3)], axis=1)
        return dot(with_edge, tw_ref[block].reshape(3 * C, C))

    norm_windows(s1, 24, 6, gains_ref[0:1, :], n_refs.at[0])
    activate(0, [(0, 768), (768, 768)], a1, slope1)
    for first, count in ((0, 11), (11, 10)):
        s2[frames(first, count), :] = s1[frames(first + 3, count), :] + temporal(
            a1, first + 3, count, 0
        )
    norm_windows(s2, 21, 3, gains_ref[1:2, :], n_refs.at[1])
    activate(1, [(0, 672), (672, 672)], a2, slope2)
    low[frames(0, 17), :] = (s2[frames(2, 17), :] + temporal(a2, 2, 17, 1)).astype(BF16)
    low[frames(17, 1), :] = jnp.zeros((PIX, C), BF16)

    pairs = low[...].reshape(9, 2 * PIX, C)
    taps = jnp.concatenate(
        [
            pairs[1:9, :PIX].reshape(8 * PIX, C),
            pairs[0:8, PIX:].reshape(8 * PIX, C),
            pairs[0:8, :PIX].reshape(8 * PIX, C),
        ],
        axis=1,
    )
    one_hot = place_matrix(32)
    down = dot(taps, rw_ref[...].reshape(3 * C, C)).astype(BF16).astype(F32)
    down = down.reshape(32, 16, C)
    for i in range(2):
        both = dot_tn(one_hot, down[:, i * 8 : (i + 1) * 8].reshape(256, C).astype(BF16))
        for j in range(2):
            tap = 2 * i + j
            enc_ref[:, tap * C : (tap + 1) * C] = both[j * 128 : (j + 1) * 128].astype(BF16)
    cotf[frames(0, 8), :] = ungroup(cot_ref, 32, one_hot)
    cotf[frames(8, 3), :] = ungroup(cot_after_ref, 12, place_matrix(12))
    grad_down = dot_tn(taps, cotf[frames(0, 8), :])
    for k in range(3):
        put(24 + k, grad_down[k * C : (k + 1) * C])
    even = dot_nt(cotf[frames(0, 10), :], rw_ref[1])
    odd = dot_nt(cotf[frames(0, 10), :], rw_ref[0]) + dot_nt(cotf[frames(1, 10), :], rw_ref[2])
    merged = jnp.concatenate(
        [even.reshape(10, PIX, C), odd.reshape(10, PIX, C)], axis=1
    ).reshape(20 * PIX, C)
    up[...] = merged[: 18 * PIX]
    g2[...] = merged.astype(BF16)

    def block_back(block, grad, act, own, slope, count, pieces):
        with_edge = jnp.concatenate([act[frames(own - k, FR), :] for k in range(3)], axis=1)
        grad_time = dot_tn(with_edge, grad[frames(0, FR), :])
        for k in range(3):
            put(18 + 3 * block + k, grad_time[k * C : (k + 1) * C])
        for k in range(3):
            wcat[:, k * C : (k + 1) * C] = tw_ref[block, k]
        for first, size in pieces:
            later = jnp.concatenate(
                [grad[pl.ds(first + k * PIX, size), :] for k in range(3)], axis=1
            )
            ga[pl.ds(first, size), :] = dot_nt(later, wcat[:, : 3 * C])

        def body(index, _):
            rows = one_frame(index)
            write_windows(ga[rows, :] * slope[one_frame(index + own), :], im, rows, -1)
            return 0

        lax.fori_loop(0, count, body, 0)
        for tap in range(9):
            wcat[:, tap * C : (tap + 1) * C] = sw_ref[block, tap]
        for first, size in pieces:
            gn[pl.ds(first, size), :] = dot_nt(im[pl.ds(first, size), :], wcat[...])
        for i in range(3):
            grad_sp = dot_tn(n_refs[block], im[frames(0, FR), 3 * i * C : 3 * (i + 1) * C])
            for j in range(3):
                put(9 * block + 3 * i + j, grad_sp[:, j * C : (j + 1) * C])

    def gain_part(index, src, own):
        value = src[one_frame(index + own), :]
        inv = lax.rsqrt(jnp.mean(value * value, axis=-1, keepdims=True) + EPSILON)
        unit = value * inv
        grad = gn[one_frame(index), :]
        return grad, unit, inv

    block_back(1, g2, a2, 3, slope2, 18, [(0, 576), (576, 576)])
    gain = gains_ref[1:2, :]

    def norm_back(index, total):
        grad, unit, inv = gain_part(index, s2, 3)
        scaled = grad * gain
        back = inv * (scaled - unit * jnp.mean(unit * scaled, axis=-1, keepdims=True))
        rows = one_frame(index)
        g1[rows, :] = (up[rows, :] + back).astype(BF16)
        return total + jnp.sum((grad * unit).reshape(8, 8, C), axis=0)

    none = jnp.zeros((8, C), F32)
    total2 = lax.fori_loop(0, FR, norm_back, none)
    lax.fori_loop(FR, FR + 2, norm_back, none)

    block_back(0, g1, a1, 6, slope1, 16, [(0, 512), (512, 512)])

    def gain_only(index, total):
        grad, unit, _ = gain_part(index, s1, 6)
        return total + jnp.sum((grad * unit).reshape(8, 8, C), axis=0)

    total1 = lax.fori_loop(0, FR, gain_only, none)
    rest = jnp.concatenate(
        [
            jnp.sum(total1, axis=0, keepdims=True),
            jnp.sum(total2, axis=0, keepdims=True),
            jnp.zeros((14, C), F32),
        ],
        axis=0,
    )
    for half in range(2):
        grad_ref[half, ROWS : ROWS + 16, :] = rest[:, half * 128 : (half + 1) * 128].astype(BF16)
        grad_ref[half, ROWS + 16 :, :] = jnp.zeros((FLAT - ROWS - 16, 128), BF16)


def run_model(video, before, after, cot, cot_after, gains, sw, tw, rw):
    def vm(rows, dtype, cols=C):
        return pltpu.VMEM((rows * PIX, cols), dtype)

    whole = pl.BlockSpec(memory_space=pltpu.VMEM)
    return pl.pallas_call(
        model_kernel,
        out_shape=(
            jax.ShapeDtypeStruct((128, 4 * C), BF16),
            jax.ShapeDtypeStruct((2, FLAT, 128), BF16),
        ),
        in_specs=[whole] * 9,
        out_specs=(whole, whole),
        scratch_shapes=[
            vm(24, F32),
            vm(21, F32),
            vm(24, BF16, 9 * C),
            pltpu.VMEM((2, FR * PIX, C), BF16),
            vm(24, BF16),
            vm(21, BF16),
            vm(24, F32),
            vm(21, F32),
            vm(18, BF16),
            vm(11, BF16),
            vm(18, F32),
            vm(20, BF16),
            vm(18, BF16),
            vm(18, F32),
            vm(18, F32),
            pltpu.VMEM((C, 9 * C), BF16),
        ],
        compiler_params=pltpu.CompilerParams(vmem_limit_bytes=56 * 1024 * 1024),
        cost_estimate=pl.CostEstimate(
            flops=12_000_000_000, bytes_accessed=10_000_000, transcendentals=1_000_000
        ),
    )(video, before, after, cot, cot_after, gains, sw, tw, rw)


def passed_along(value, axes, steps):
    count = lax.axis_size(axes)
    first, last = (max(0, -steps), min(count, count - steps))
    return lax.ppermute(value, axes, [(source, source + steps) for source in range(first, last)])


def exchange(value, axes):
    return lax.all_to_all(value, axes, split_axis=0, concat_axis=0, tiled=True)


def to_all(value, axes, count):
    rows, cols = value.shape
    copies = jnp.broadcast_to(value[None], (count, rows, cols)).reshape(count * rows, cols)
    return exchange(copies, axes)


def on_device(video, cotangent, gains, spatial_weights, time_weights, reduce_kernel_weights):
    tm = ("z", "xl")
    video = video.reshape(FR * PIX, C)
    cot = cotangent.reshape(FR * 8, 4 * C)
    before = passed_along(video[-6 * PIX :], tm, 1)
    after = passed_along(video[: 2 * PIX], tm, -1)
    cot_after = passed_along(cot[: 3 * 16], tm, -1)
    encoded, grads = run_model(
        video,
        before,
        after,
        cot,
        cot_after,
        gains,
        spatial_weights.reshape(2, 9, C, C),
        time_weights,
        reduce_kernel_weights,
    )
    core = lax.axis_index("core")
    swap = [(0, 1), (1, 0)]
    mine = jnp.where(core == 0, grads[0], grads[1])
    other = lax.ppermute(jnp.where(core == 0, grads[1], grads[0]), "core", swap)
    half = (mine.astype(F32) + other.astype(F32)).astype(BF16)
    parts = exchange(half, PLANE).reshape(16, CHUNK, 128)
    part = jnp.sum(parts.astype(F32), axis=0).astype(BF16)
    parts = to_all(part, "z", 8).reshape(8, CHUNK, 128)
    part = jnp.sum(parts.astype(F32), axis=0).astype(BF16)
    mine = to_all(part, PLANE, 16)
    other = lax.ppermute(mine, "core", swap)
    left = jnp.where(core == 0, mine, other)
    right = jnp.where(core == 0, other, mine)
    full = jnp.concatenate([left, right], axis=1).astype(F32)
    return (
        encoded.reshape(1, FR // 2, 4, 4, 4 * C),
        full[: 18 * C].reshape(2, 3, 3, C, C),
        full[18 * C : 24 * C].reshape(2, 3, C, C),
        full[24 * C : ROWS].reshape(3, C, C),
        full[ROWS : ROWS + 2],
    )


def solution(mesh):
    fine = Mesh(mesh.devices.reshape(2, 4, 2, 8, 2), EVERY)
    split = P(("xh", "y", "core"), ("z", "xl"), None, None, None)
    return jax.shard_map(
        on_device,
        mesh=fine,
        in_specs=(split, split, P(), P(), P(), P()),
        out_specs=(split, P(), P(), P(), P()),
        check_vma=False,
    )
```

```python
import jax
import jax.numpy as jnp
from jax import lax
from jax.experimental import pallas as pl
from jax.experimental.pallas import tpu as pltpu
from jax.sharding import Mesh, PartitionSpec as P

EPSILON = 1e-06
F32 = jnp.float32
BF16 = jnp.bfloat16
C = 256
PIX = 64
FR = 16
UNROLL = 2
OUT = pltpu.VMEM
HBM = pltpu.HBM
MATS = 27
ROWS = MATS * C
CHUNK = 448
FLAT = 16 * CHUNK
EVERY = ("xh", "y", "core", "z", "xl")
PLANE = ("xh", "xl", "y")


def dot(left, right):
    return jnp.dot(left, right, preferred_element_type=F32)


def dot_nt(left, right):
    return lax.dot_general(left, right, (((1,), (1,)), ((), ())), preferred_element_type=F32)


def dot_tn(left, right):
    return lax.dot_general(left, right, (((0,), (0,)), ((), ())), preferred_element_type=F32)


def frames(first, count):
    return pl.ds(first * PIX, count * PIX)


def one_frame(index):
    return pl.ds(pl.multiple_of(index * PIX, PIX), PIX)


def write_windows(value, im_ref, rows, sign):
    grid = value.reshape(8, 8, C)
    column = lax.broadcasted_iota(jnp.int32, (8, 8, C), 1)
    blank = jnp.zeros((1, 8, C), F32)
    for j in range(3):
        dx = sign * (j - 1)
        if dx == 0:
            moved = grid
        elif dx == 1:
            moved = jnp.where(column == 7, 0.0, pltpu.roll(grid, 7, 1))
        else:
            moved = jnp.where(column == 0, 0.0, pltpu.roll(grid, 1, 1))
        for i in range(3):
            dy = sign * (i - 1)
            if dy == 0:
                placed = moved
            elif dy == 1:
                placed = jnp.concatenate([moved[1:], blank], axis=0)
            else:
                placed = jnp.concatenate([blank, moved[:-1]], axis=0)
            tap = 3 * i + j
            im_ref[rows, tap * C : (tap + 1) * C] = placed.reshape(PIX, C).astype(BF16)


def place_matrix(groups):
    size = groups * 8
    dest = lax.broadcasted_iota(jnp.int32, (size, size), 0)
    src = lax.broadcasted_iota(jnp.int32, (size, size), 1)
    want = (dest & 1) * (groups * 4) + (dest >> 3) * 4 + ((dest >> 1) & 3)
    return jnp.where(src == want, 1.0, 0.0).astype(BF16)


def ungroup(piece, groups, one_hot):
    halves = []
    for i in range(2):
        both = jnp.concatenate([piece(2 * i + j) for j in range(2)], axis=0)
        halves.append(dot(one_hot, both).reshape(groups, 8, C))
    return jnp.concatenate(halves, axis=1).reshape(groups * 16, C).astype(BF16)


def norm_windows(src, first, count, gain, im, n_ref=None):
    def body(index, _):
        rows = one_frame(index)
        value = src[one_frame(index + first), :].astype(F32)
        inv = lax.rsqrt(jnp.mean(value * value, axis=-1, keepdims=True) + EPSILON)
        value = value * inv * gain
        write_windows(value, im, rows, 1)
        if n_ref is not None:
            n_ref[rows, :] = value.astype(BF16)
        return 0

    lax.fori_loop(0, count, body, 0, unroll=UNROLL)


def activate(im, weights, pieces, act, slope):
    for first, size, act_first, slope_first in pieces:
        conv = dot(im[pl.ds(first, size), :], weights.reshape(9 * C, C))
        logistic = jax.nn.sigmoid(conv)
        act[pl.ds(act_first, size), :] = (conv * logistic).astype(BF16)
        if slope_first is not None:
            slope[pl.ds(slope_first, size), :] = logistic * (1.0 + conv * (1.0 - logistic))


def front_kernel(
    video_hbm, gains_hbm, sw_hbm, n_ref, act_ref, slope_ref, im, video, gains, weights, sems
):
    copies = [
        pltpu.make_async_copy(video_hbm, video, sems.at[0]),
        pltpu.make_async_copy(gains_hbm, gains, sems.at[1]),
        pltpu.make_async_copy(sw_hbm.at[0], weights, sems.at[2]),
    ]
    for copy in copies:
        copy.start()
    copies[0].wait()
    copies[1].wait()
    norm_windows(video, 0, FR, gains[0:1, :], im, n_ref)
    copies[2].wait()
    activate(im, weights[...], [(0, 512, 0, 0), (512, 512, 512, 512)], act_ref, slope_ref)


def model_kernel(
    core_ref,
    n1_ref,
    a1_ref,
    slope1,
    before_ref,
    after_ref,
    cot_ref,
    video_hbm,
    gains_hbm,
    sw_hbm,
    tw_hbm,
    rw_hbm,
    enc_ref,
    mine_ref,
    theirs_ref,
    s1,
    s2,
    im,
    n2_ref,
    a1,
    a2,
    slope2,
    low,
    cotf,
    up,
    g2,
    g1,
    ga,
    gn,
    wcat,
    video,
    gains_ref,
    sw_ref,
    tw_ref,
    rw_ref,
    sems,
):
    pairs = [
        (gains_hbm, gains_ref),
        (sw_hbm.at[0], sw_ref.at[0]),
        (video_hbm, video),
        (tw_hbm, tw_ref),
        (sw_hbm.at[1], sw_ref.at[1]),
        (rw_hbm, rw_ref),
    ]
    copies = [pltpu.make_async_copy(*pair, sems.at[i]) for i, pair in enumerate(pairs)]
    for copy in copies:
        copy.start()
    s1[frames(0, 6), :] = before_ref[...].astype(F32)
    s1[frames(22, 2), :] = after_ref[: 2 * PIX].astype(F32)
    a1[frames(6, 16), :] = a1_ref[...]
    n_refs = (n1_ref, n2_ref)
    first_core = core_ref[0] == 0

    def put_halves(rows, value):
        low_half = value[:, :128].astype(BF16)
        high_half = value[:, 128:].astype(BF16)
        mine_ref[rows, :] = jnp.where(first_core, low_half, high_half)
        theirs_ref[rows, :] = jnp.where(first_core, high_half, low_half)

    def put(matrix, value):
        put_halves(pl.ds(matrix * C, C), value)

    def temporal(act, first, count, block):
        with_edge = jnp.concatenate([act[frames(first - k, count), :] for k in range(3)], axis=1)
        return dot(with_edge, tw_ref[block].reshape(3 * C, C))

    copies[0].wait()
    norm_windows(s1, 0, 6, gains_ref[0:1, :], im)
    norm_windows(s1, 22, 2, gains_ref[0:1, :], im.at[frames(6, 2)])
    copies[1].wait()
    activate(im, sw_ref[0], [(0, 384, 0, None), (384, 128, 1408, None)], a1, None)
    copies[2].wait()
    s1[frames(6, 16), :] = video[...].astype(F32)
    copies[3].wait()
    for first, count in ((0, 11), (11, 10)):
        s2[frames(first, count), :] = s1[frames(first + 3, count), :] + temporal(
            a1, first + 3, count, 0
        )
    norm_windows(s2, 0, 3, gains_ref[1:2, :], im)
    norm_windows(s2, 3, 16, gains_ref[1:2, :], im.at[frames(3, 16)], n2_ref)
    norm_windows(s2, 19, 2, gains_ref[1:2, :], im.at[frames(19, 2)])
    copies[4].wait()
    activate(im, sw_ref[1], [(0, 672, 0, 0), (672, 672, 672, 672)], a2, slope2)
    copies[5].wait()
    low[frames(0, 17), :] = (s2[frames(2, 17), :] + temporal(a2, 2, 17, 1)).astype(BF16)
    low[frames(17, 1), :] = jnp.zeros((PIX, C), BF16)

    pairs = low[...].reshape(9, 2 * PIX, C)
    taps = jnp.concatenate(
        [
            pairs[1:9, :PIX].reshape(8 * PIX, C),
            pairs[0:8, PIX:].reshape(8 * PIX, C),
            pairs[0:8, :PIX].reshape(8 * PIX, C),
        ],
        axis=1,
    )
    one_hot = place_matrix(32)
    down = dot(taps, rw_ref[...].reshape(3 * C, C)).astype(BF16).astype(F32)
    down = down.reshape(32, 16, C)
    for i in range(2):
        both = dot_tn(one_hot, down[:, i * 8 : (i + 1) * 8].reshape(256, C).astype(BF16))
        for j in range(2):
            tap = 2 * i + j
            enc_ref[:, tap * C : (tap + 1) * C] = both[j * 128 : (j + 1) * 128].astype(BF16)
    cotf[frames(0, 8), :] = ungroup(
        lambda tap: cot_ref[:, tap * C : (tap + 1) * C], 32, one_hot
    )
    cotf[frames(8, 3), :] = ungroup(
        lambda tap: after_ref[2 * PIX + tap * 48 : 2 * PIX + (tap + 1) * 48, :],
        12,
        place_matrix(12),
    )
    grad_down = dot_tn(taps, cotf[frames(0, 8), :])
    for k in range(3):
        put(24 + k, grad_down[k * C : (k + 1) * C])
    even = dot_nt(cotf[frames(0, 10), :], rw_ref[1])
    odd = dot_nt(cotf[frames(0, 10), :], rw_ref[0]) + dot_nt(cotf[frames(1, 10), :], rw_ref[2])
    merged = jnp.concatenate(
        [even.reshape(10, PIX, C), odd.reshape(10, PIX, C)], axis=1
    ).reshape(20 * PIX, C)
    up[...] = merged[: 18 * PIX]
    g2[...] = merged.astype(BF16)

    def block_back(block, grad, act, own, slope, slope_own, count, pieces):
        with_edge = jnp.concatenate([act[frames(own - k, FR), :] for k in range(3)], axis=1)
        grad_time = dot_tn(with_edge, grad[frames(0, FR), :])
        for k in range(3):
            put(18 + 3 * block + k, grad_time[k * C : (k + 1) * C])
        for k in range(3):
            wcat[:, k * C : (k + 1) * C] = tw_ref[block, k]
        for first, size in pieces:
            later = jnp.concatenate(
                [grad[pl.ds(first + k * PIX, size), :] for k in range(3)], axis=1
            )
            ga[pl.ds(first, size), :] = dot_nt(later, wcat[:, : 3 * C])

        def body(index, _):
            rows = one_frame(index)
            write_windows(ga[rows, :] * slope[one_frame(index + slope_own), :], im, rows, -1)
            return 0

        lax.fori_loop(0, count, body, 0, unroll=UNROLL)
        for tap in range(9):
            wcat[:, tap * C : (tap + 1) * C] = sw_ref[block, tap]
        for first, size in pieces:
            gn[pl.ds(first, size), :] = dot_nt(im[pl.ds(first, size), :], wcat[...])
        for i in range(3):
            grad_sp = dot_tn(n_refs[block][...], im[frames(0, FR), 3 * i * C : 3 * (i + 1) * C])
            for j in range(3):
                put(9 * block + 3 * i + j, grad_sp[:, j * C : (j + 1) * C])

    def gain_part(index, src, own):
        value = src[one_frame(index + own), :]
        inv = lax.rsqrt(jnp.mean(value * value, axis=-1, keepdims=True) + EPSILON)
        unit = value * inv
        grad = gn[one_frame(index), :]
        return grad, unit, inv

    block_back(1, g2, a2, 3, slope2, 3, 18, [(0, 576), (576, 576)])
    gain = gains_ref[1:2, :]

    def norm_back(index, total):
        grad, unit, inv = gain_part(index, s2, 3)
        scaled = grad * gain
        back = inv * (scaled - unit * jnp.mean(unit * scaled, axis=-1, keepdims=True))
        rows = one_frame(index)
        g1[rows, :] = (up[rows, :] + back).astype(BF16)
        return total + jnp.sum((grad * unit).reshape(8, 8, C), axis=0)

    none = jnp.zeros((8, C), F32)
    total2 = lax.fori_loop(0, FR, norm_back, none, unroll=UNROLL)
    lax.fori_loop(FR, FR + 2, norm_back, none)

    block_back(0, g1, a1, 6, slope1, 0, 16, [(0, 512), (512, 512)])

    def gain_only(index, total):
        grad, unit, _ = gain_part(index, s1, 6)
        return total + jnp.sum((grad * unit).reshape(8, 8, C), axis=0)

    total1 = lax.fori_loop(0, FR, gain_only, none, unroll=UNROLL)
    rest = jnp.concatenate(
        [
            jnp.sum(total1, axis=0, keepdims=True),
            jnp.sum(total2, axis=0, keepdims=True),
            jnp.zeros((14, C), F32),
        ],
        axis=0,
    )
    put_halves(pl.ds(ROWS, 16), rest)
    for ref in (mine_ref, theirs_ref):
        ref[ROWS + 16 :, :] = jnp.zeros((FLAT - ROWS - 16, 128), BF16)


def run_model(core, video, before, after, cot, gains, sw, tw, rw):
    def vm(rows, dtype, cols=C):
        return pltpu.VMEM((rows * PIX, cols), dtype)

    whole = pl.BlockSpec(memory_space=pltpu.VMEM)
    hbm = pl.BlockSpec(memory_space=HBM)
    normed, act, slope = pl.pallas_call(
        front_kernel,
        out_shape=(OUT((FR * PIX, C), BF16), OUT((FR * PIX, C), BF16), OUT((FR * PIX, C), F32)),
        in_specs=[hbm] * 3,
        out_specs=(whole,) * 3,
        scratch_shapes=[
            vm(16, BF16, 9 * C),
            vm(16, BF16),
            pltpu.VMEM((2, C), F32),
            pltpu.VMEM((9, C, C), BF16),
            pltpu.SemaphoreType.DMA((3,)),
        ],
        compiler_params=pltpu.CompilerParams(vmem_limit_bytes=24 * 1024 * 1024),
        cost_estimate=pl.CostEstimate(
            flops=1_200_000_000, bytes_accessed=4_000_000, transcendentals=500_000
        ),
    )(video, gains, sw)
    return pl.pallas_call(
        model_kernel,
        out_shape=(
            jax.ShapeDtypeStruct((128, 4 * C), BF16),
            OUT((FLAT, 128), BF16),
            OUT((FLAT, 128), BF16),
        ),
        in_specs=[pl.BlockSpec(memory_space=pltpu.SMEM)] + [whole] * 6 + [hbm] * 5,
        out_specs=(whole, whole, whole),
        scratch_shapes=[
            vm(24, F32),
            vm(21, F32),
            vm(21, BF16, 9 * C),
            vm(16, BF16),
            vm(24, BF16),
            vm(21, BF16),
            vm(21, F32),
            vm(18, BF16),
            vm(11, BF16),
            vm(18, F32),
            vm(20, BF16),
            vm(18, BF16),
            vm(18, F32),
            vm(18, F32),
            pltpu.VMEM((C, 9 * C), BF16),
            vm(16, BF16),
            pltpu.VMEM((2, C), F32),
            pltpu.VMEM((2, 9, C, C), BF16),
            pltpu.VMEM((2, 3, C, C), BF16),
            pltpu.VMEM((3, C, C), BF16),
            pltpu.SemaphoreType.DMA((6,)),
        ],
        compiler_params=pltpu.CompilerParams(vmem_limit_bytes=40 * 1024 * 1024),
        cost_estimate=pl.CostEstimate(
            flops=10_000_000_000, bytes_accessed=8_000_000, transcendentals=1_000_000
        ),
    )(core, normed, act, slope, before, after, cot, video, gains, sw, tw, rw)


def passed_along(value, axes, steps):
    count = lax.axis_size(axes)
    first, last = (max(0, -steps), min(count, count - steps))
    return lax.ppermute(value, axes, [(source, source + steps) for source in range(first, last)])


def exchange(value, axes):
    return lax.all_to_all(value, axes, split_axis=0, concat_axis=0, tiled=True)


def to_all(value, axes, count):
    rows, cols = value.shape
    copies = jnp.broadcast_to(value[None], (count, rows, cols)).reshape(count * rows, cols)
    return exchange(copies, axes)


def place_kernel(core_ref, part_ref, *refs):
    sp_ref, tm_ref, dn_ref, gn_ref, buf, gains, sems = refs[-7:]
    lanes = pl.ds(pl.multiple_of(core_ref[0] * 128, 128), 128)
    copies = []
    for matrix in range(MATS):
        buf[matrix] = part_ref[pl.ds(matrix * C, C), :].astype(F32)
        if matrix < 18:
            target = sp_ref.at[matrix, :, lanes]
        elif matrix < 24:
            target = tm_ref.at[matrix - 18, :, lanes]
        else:
            target = dn_ref.at[matrix - 24, :, lanes]
        copies.append(pltpu.make_async_copy(buf.at[matrix], target, sems.at[matrix]))
        copies[-1].start()
    gains[...] = part_ref[ROWS : ROWS + 16, :].astype(F32)[:8]
    copies.append(pltpu.make_async_copy(gains, gn_ref.at[:, lanes], sems.at[MATS]))
    copies[-1].start()
    for copy in copies:
        copy.wait()


def place(which, part, outputs=()):
    whole = pl.BlockSpec(memory_space=pltpu.VMEM)
    hbm = pl.BlockSpec(memory_space=HBM)
    return pl.pallas_call(
        place_kernel,
        out_shape=(
            jax.ShapeDtypeStruct((18, C, C), F32),
            jax.ShapeDtypeStruct((6, C, C), F32),
            jax.ShapeDtypeStruct((3, C, C), F32),
            jax.ShapeDtypeStruct((8, C), F32),
        ),
        in_specs=[pl.BlockSpec(memory_space=pltpu.SMEM), whole] + [hbm] * len(outputs),
        out_specs=(hbm,) * 4,
        scratch_shapes=[
            pltpu.VMEM((MATS, C, 128), F32),
            pltpu.VMEM((8, 128), F32),
            pltpu.SemaphoreType.DMA((MATS + 1,)),
        ],
        input_output_aliases={2 + i: i for i in range(len(outputs))},
        compiler_params=pltpu.CompilerParams(vmem_limit_bytes=16 * 1024 * 1024),
        cost_estimate=pl.CostEstimate(flops=0, bytes_accessed=6_000_000, transcendentals=0),
    )(which, part, *outputs)


def on_device(video, cotangent, gains, spatial_weights, time_weights, reduce_kernel_weights):
    tm = ("z", "xl")
    video = video.reshape(FR * PIX, C)
    cot = cotangent.reshape(FR * 8, 4 * C)
    before = passed_along(video[-6 * PIX :], tm, 1)
    leading = [video[: 2 * PIX]] + [cot[:48, tap * C : (tap + 1) * C] for tap in range(4)]
    after = passed_along(jnp.concatenate(leading, axis=0), tm, -1)
    core = lax.axis_index("core").astype(jnp.int32).reshape(1)
    encoded, mine, theirs = run_model(
        core,
        video,
        before,
        after,
        cot,
        gains,
        spatial_weights.reshape(2, 9, C, C),
        time_weights,
        reduce_kernel_weights,
    )
    swap = [(0, 1), (1, 0)]
    other = lax.ppermute(theirs, "core", swap)
    half = (mine.astype(F32) + other.astype(F32)).astype(BF16)
    parts = exchange(half, PLANE).reshape(16, CHUNK, 128)
    part = jnp.sum(parts.astype(F32), axis=0).astype(BF16)
    parts = exchange(part, "z").reshape(8, CHUNK // 8, 128)
    part = jnp.sum(parts.astype(F32), axis=0).astype(BF16)
    part = to_all(part, "z", 8)
    mine = to_all(part, PLANE, 16)
    other = lax.ppermute(mine, "core", swap)
    outputs = place(core, mine)
    grad_sp, grad_tm, grad_dn, grad_gn = place(1 - core, other, outputs)
    return (
        encoded.reshape(1, FR // 2, 4, 4, 4 * C),
        grad_sp.reshape(2, 3, 3, C, C),
        grad_tm.reshape(2, 3, C, C),
        grad_dn,
        grad_gn[:2],
    )


def solution(mesh):
    fine = Mesh(mesh.devices.reshape(2, 4, 2, 8, 2), EVERY)
    split = P(("xh", "y", "core"), ("z", "xl"), None, None, None)
    return jax.shard_map(
        on_device,
        mesh=fine,
        in_specs=(split, split, P(), P(), P(), P()),
        out_specs=(split, P(), P(), P(), P()),
        check_vma=False,
    )
```

```python
import jax
import jax.numpy as jnp
from jax import lax
from jax.experimental import pallas as pl
from jax.experimental.pallas import tpu as pltpu
from jax.sharding import Mesh, PartitionSpec as P

EPSILON = 1e-06
F32 = jnp.float32
BF16 = jnp.bfloat16
C = 256
PIX = 64
FR = 16
OUT = pltpu.VMEM
HBM = pltpu.HBM
MATS = 27
ROWS = MATS * C
CHUNK = 448
FLAT = 16 * CHUNK
EVERY = ("xh", "y", "core", "zh", "zl", "xl")
PLANE = ("xh", "xl", "y", "zl")


def dot(left, right):
    return jnp.dot(left, right, preferred_element_type=F32)


def dot_nt(left, right):
    return lax.dot_general(left, right, (((1,), (1,)), ((), ())), preferred_element_type=F32)


def dot_tn(left, right):
    return lax.dot_general(left, right, (((0,), (0,)), ((), ())), preferred_element_type=F32)


def frames(first, count):
    return pl.ds(first * PIX, count * PIX)


def one_frame(index):
    return pl.ds(pl.multiple_of(index * PIX, PIX), PIX)


def write_windows(value, im_ref, rows, sign):
    grid = value.reshape(8, 8, C)
    column = lax.broadcasted_iota(jnp.int32, (8, 8, C), 1)
    blank = jnp.zeros((1, 8, C), F32)
    for j in range(3):
        dx = sign * (j - 1)
        if dx == 0:
            moved = grid
        elif dx == 1:
            moved = jnp.where(column == 7, 0.0, pltpu.roll(grid, 7, 1))
        else:
            moved = jnp.where(column == 0, 0.0, pltpu.roll(grid, 1, 1))
        for i in range(3):
            dy = sign * (i - 1)
            if dy == 0:
                placed = moved
            elif dy == 1:
                placed = jnp.concatenate([moved[1:], blank], axis=0)
            else:
                placed = jnp.concatenate([blank, moved[:-1]], axis=0)
            tap = 3 * i + j
            im_ref[rows, tap * C : (tap + 1) * C] = placed.reshape(PIX, C).astype(BF16)


def place_matrix(groups):
    size = groups * 8
    dest = lax.broadcasted_iota(jnp.int32, (size, size), 0)
    src = lax.broadcasted_iota(jnp.int32, (size, size), 1)
    want = (dest & 1) * (groups * 4) + (dest >> 3) * 4 + ((dest >> 1) & 3)
    return jnp.where(src == want, 1.0, 0.0).astype(BF16)


def ungroup(piece, groups, one_hot):
    halves = []
    for i in range(2):
        both = jnp.concatenate([piece(2 * i + j) for j in range(2)], axis=0)
        halves.append(dot(one_hot, both).reshape(groups, 8, C))
    return jnp.concatenate(halves, axis=1).reshape(groups * 16, C).astype(BF16)


def norm_windows(src, first, count, gain, im, n_ref=None):
    def body(index, _):
        rows = one_frame(index)
        value = src[one_frame(index + first), :].astype(F32)
        inv = lax.rsqrt(jnp.mean(value * value, axis=-1, keepdims=True) + EPSILON)
        value = value * inv * gain
        write_windows(value, im, rows, 1)
        if n_ref is not None:
            n_ref[rows, :] = value.astype(BF16)
        return 0

    lax.fori_loop(0, count, body, 0, unroll=True)


def activate(im, weights, pieces, act, slope):
    for first, size, act_first, slope_first in pieces:
        conv = dot(im[pl.ds(first, size), :], weights.reshape(9 * C, C))
        logistic = jax.nn.sigmoid(conv)
        act[pl.ds(act_first, size), :] = (conv * logistic).astype(BF16)
        if slope_first is not None:
            slope[pl.ds(slope_first, size), :] = logistic * (1.0 + conv * (1.0 - logistic))


def front_kernel(
    video_hbm, gains_hbm, sw_hbm, n_ref, act_ref, slope_ref, im, video, gains, weights, sems
):
    copies = [
        pltpu.make_async_copy(video_hbm, video, sems.at[0]),
        pltpu.make_async_copy(gains_hbm, gains, sems.at[1]),
        pltpu.make_async_copy(sw_hbm.at[0], weights, sems.at[2]),
    ]
    for copy in copies:
        copy.start()
    copies[0].wait()
    copies[1].wait()
    norm_windows(video, 0, FR, gains[0:1, :], im, n_ref)
    copies[2].wait()
    activate(im, weights[...], [(0, 512, 0, 0), (512, 512, 512, 512)], act_ref, slope_ref)


def model_kernel(
    core_ref,
    n1_ref,
    a1_ref,
    slope1,
    before_ref,
    after_ref,
    cot_ref,
    video_hbm,
    gains_hbm,
    sw_hbm,
    tw_hbm,
    rw_hbm,
    enc_ref,
    mine_ref,
    theirs_ref,
    s1,
    s2,
    im,
    n2_ref,
    a1,
    a2,
    slope2,
    low,
    cotf,
    up,
    g2,
    g1,
    ga,
    gn,
    wcat,
    video,
    gains_ref,
    sw_ref,
    tw_ref,
    rw_ref,
    sems,
):
    pairs = [
        (gains_hbm, gains_ref),
        (sw_hbm.at[0], sw_ref.at[0]),
        (video_hbm, video),
        (tw_hbm, tw_ref),
        (sw_hbm.at[1], sw_ref.at[1]),
        (rw_hbm, rw_ref),
    ]
    copies = [pltpu.make_async_copy(*pair, sems.at[i]) for i, pair in enumerate(pairs)]
    for copy in copies:
        copy.start()
    s1[frames(0, 6), :] = before_ref[...].astype(F32)
    s1[frames(22, 2), :] = after_ref[: 2 * PIX].astype(F32)
    a1[frames(6, 16), :] = a1_ref[...]
    n_refs = (n1_ref, n2_ref)
    first_core = core_ref[0] == 0

    def put_halves(rows, value):
        low_half = value[:, :128].astype(BF16)
        high_half = value[:, 128:].astype(BF16)
        mine_ref[rows, :] = jnp.where(first_core, low_half, high_half)
        theirs_ref[rows, :] = jnp.where(first_core, high_half, low_half)

    def put(matrix, value):
        put_halves(pl.ds(matrix * C, C), value)

    def temporal(act, first, count, block):
        with_edge = jnp.concatenate([act[frames(first - k, count), :] for k in range(3)], axis=1)
        return dot(with_edge, tw_ref[block].reshape(3 * C, C))

    copies[0].wait()
    norm_windows(s1, 0, 6, gains_ref[0:1, :], im)
    norm_windows(s1, 22, 2, gains_ref[0:1, :], im.at[frames(6, 2)])
    copies[1].wait()
    activate(im, sw_ref[0], [(0, 384, 0, None), (384, 128, 1408, None)], a1, None)
    copies[2].wait()
    s1[frames(6, 16), :] = video[...].astype(F32)
    copies[3].wait()
    for first, count in ((0, 11), (11, 10)):
        s2[frames(first, count), :] = s1[frames(first + 3, count), :] + temporal(
            a1, first + 3, count, 0
        )
    norm_windows(s2, 0, 3, gains_ref[1:2, :], im)
    norm_windows(s2, 3, 16, gains_ref[1:2, :], im.at[frames(3, 16)], n2_ref)
    norm_windows(s2, 19, 2, gains_ref[1:2, :], im.at[frames(19, 2)])
    copies[4].wait()
    activate(im, sw_ref[1], [(0, 672, 0, 0), (672, 672, 672, 672)], a2, slope2)
    copies[5].wait()
    low[frames(0, 17), :] = (s2[frames(2, 17), :] + temporal(a2, 2, 17, 1)).astype(BF16)
    low[frames(17, 1), :] = jnp.zeros((PIX, C), BF16)

    pairs = low[...].reshape(9, 2 * PIX, C)
    taps = jnp.concatenate(
        [
            pairs[1:9, :PIX].reshape(8 * PIX, C),
            pairs[0:8, PIX:].reshape(8 * PIX, C),
            pairs[0:8, :PIX].reshape(8 * PIX, C),
        ],
        axis=1,
    )
    one_hot = place_matrix(32)
    down = dot(taps, rw_ref[...].reshape(3 * C, C)).astype(BF16).astype(F32)
    down = down.reshape(32, 16, C)
    for i in range(2):
        both = dot_tn(one_hot, down[:, i * 8 : (i + 1) * 8].reshape(256, C).astype(BF16))
        for j in range(2):
            tap = 2 * i + j
            enc_ref[:, tap * C : (tap + 1) * C] = both[j * 128 : (j + 1) * 128].astype(BF16)
    cotf[frames(0, 8), :] = ungroup(
        lambda tap: cot_ref[:, tap * C : (tap + 1) * C], 32, one_hot
    )
    cotf[frames(8, 3), :] = ungroup(
        lambda tap: after_ref[2 * PIX + tap * 48 : 2 * PIX + (tap + 1) * 48, :],
        12,
        place_matrix(12),
    )
    grad_down = dot_tn(taps, cotf[frames(0, 8), :])
    for k in range(3):
        put(24 + k, grad_down[k * C : (k + 1) * C])
    even = dot_nt(cotf[frames(0, 10), :], rw_ref[1])
    odd = dot_nt(cotf[frames(0, 10), :], rw_ref[0]) + dot_nt(cotf[frames(1, 10), :], rw_ref[2])
    merged = jnp.concatenate(
        [even.reshape(10, PIX, C), odd.reshape(10, PIX, C)], axis=1
    ).reshape(20 * PIX, C)
    up[...] = merged[: 18 * PIX]
    g2[...] = merged.astype(BF16)

    def block_back(block, grad, act, own, slope, slope_own, count, pieces):
        with_edge = jnp.concatenate([act[frames(own - k, FR), :] for k in range(3)], axis=1)
        grad_time = dot_tn(with_edge, grad[frames(0, FR), :])
        for k in range(3):
            put(18 + 3 * block + k, grad_time[k * C : (k + 1) * C])
        for k in range(3):
            wcat[:, k * C : (k + 1) * C] = tw_ref[block, k]
        for first, size in pieces:
            later = jnp.concatenate(
                [grad[pl.ds(first + k * PIX, size), :] for k in range(3)], axis=1
            )
            ga[pl.ds(first, size), :] = dot_nt(later, wcat[:, : 3 * C])

        def body(index, _):
            rows = one_frame(index)
            write_windows(ga[rows, :] * slope[one_frame(index + slope_own), :], im, rows, -1)
            return 0

        lax.fori_loop(0, count, body, 0, unroll=True)
        for tap in range(9):
            wcat[:, tap * C : (tap + 1) * C] = sw_ref[block, tap]
        for first, size in pieces:
            gn[pl.ds(first, size), :] = dot_nt(im[pl.ds(first, size), :], wcat[...])
        for i in range(3):
            grad_sp = dot_tn(n_refs[block][...], im[frames(0, FR), 3 * i * C : 3 * (i + 1) * C])
            for j in range(3):
                put(9 * block + 3 * i + j, grad_sp[:, j * C : (j + 1) * C])

    def gain_part(index, src, own):
        value = src[one_frame(index + own), :]
        inv = lax.rsqrt(jnp.mean(value * value, axis=-1, keepdims=True) + EPSILON)
        unit = value * inv
        grad = gn[one_frame(index), :]
        return grad, unit, inv

    block_back(1, g2, a2, 3, slope2, 3, 18, [(0, 576), (576, 576)])
    gain = gains_ref[1:2, :]

    def norm_back(index, total):
        grad, unit, inv = gain_part(index, s2, 3)
        scaled = grad * gain
        back = inv * (scaled - unit * jnp.mean(unit * scaled, axis=-1, keepdims=True))
        rows = one_frame(index)
        g1[rows, :] = (up[rows, :] + back).astype(BF16)
        return total + jnp.sum((grad * unit).reshape(8, 8, C), axis=0)

    none = jnp.zeros((8, C), F32)
    total2 = lax.fori_loop(0, FR, norm_back, none, unroll=True)
    lax.fori_loop(FR, FR + 2, norm_back, none, unroll=True)

    block_back(0, g1, a1, 6, slope1, 0, 16, [(0, 512), (512, 512)])

    def gain_only(index, total):
        grad, unit, _ = gain_part(index, s1, 6)
        return total + jnp.sum((grad * unit).reshape(8, 8, C), axis=0)

    total1 = lax.fori_loop(0, FR, gain_only, none, unroll=True)
    rest = jnp.concatenate(
        [
            jnp.sum(total1, axis=0, keepdims=True),
            jnp.sum(total2, axis=0, keepdims=True),
            jnp.zeros((14, C), F32),
        ],
        axis=0,
    )
    put_halves(pl.ds(ROWS, 16), rest)
    for ref in (mine_ref, theirs_ref):
        ref[ROWS + 16 :, :] = jnp.zeros((FLAT - ROWS - 16, 128), BF16)


def run_model(core, video, before, after, cot, gains, sw, tw, rw):
    def vm(rows, dtype, cols=C):
        return pltpu.VMEM((rows * PIX, cols), dtype)

    whole = pl.BlockSpec(memory_space=pltpu.VMEM)
    hbm = pl.BlockSpec(memory_space=HBM)
    video, gains, sw, tw, rw = (
        pltpu.with_memory_space_constraint(value, HBM) for value in (video, gains, sw, tw, rw)
    )
    normed, act, slope = pl.pallas_call(
        front_kernel,
        out_shape=(OUT((FR * PIX, C), BF16), OUT((FR * PIX, C), BF16), OUT((FR * PIX, C), F32)),
        in_specs=[hbm] * 3,
        out_specs=(whole,) * 3,
        scratch_shapes=[
            vm(16, BF16, 9 * C),
            vm(16, BF16),
            pltpu.VMEM((2, C), F32),
            pltpu.VMEM((9, C, C), BF16),
            pltpu.SemaphoreType.DMA((3,)),
        ],
        compiler_params=pltpu.CompilerParams(vmem_limit_bytes=24 * 1024 * 1024),
        cost_estimate=pl.CostEstimate(
            flops=1_200_000_000, bytes_accessed=4_000_000, transcendentals=500_000
        ),
    )(video, gains, sw)
    return pl.pallas_call(
        model_kernel,
        out_shape=(
            jax.ShapeDtypeStruct((128, 4 * C), BF16),
            OUT((FLAT, 128), BF16),
            OUT((FLAT, 128), BF16),
        ),
        in_specs=[pl.BlockSpec(memory_space=pltpu.SMEM)] + [whole] * 6 + [hbm] * 5,
        out_specs=(whole, whole, whole),
        scratch_shapes=[
            vm(24, F32),
            vm(21, F32),
            vm(21, BF16, 9 * C),
            vm(16, BF16),
            vm(24, BF16),
            vm(21, BF16),
            vm(21, F32),
            vm(18, BF16),
            vm(11, BF16),
            vm(18, F32),
            vm(20, BF16),
            vm(18, BF16),
            vm(18, F32),
            vm(18, F32),
            pltpu.VMEM((C, 9 * C), BF16),
            vm(16, BF16),
            pltpu.VMEM((2, C), F32),
            pltpu.VMEM((2, 9, C, C), BF16),
            pltpu.VMEM((2, 3, C, C), BF16),
            pltpu.VMEM((3, C, C), BF16),
            pltpu.SemaphoreType.DMA((6,)),
        ],
        compiler_params=pltpu.CompilerParams(vmem_limit_bytes=40 * 1024 * 1024),
        cost_estimate=pl.CostEstimate(
            flops=10_000_000_000, bytes_accessed=8_000_000, transcendentals=1_000_000
        ),
    )(core, normed, act, slope, before, after, cot, video, gains, sw, tw, rw)


def passed_along(value, axes, steps):
    count = lax.axis_size(axes)
    first, last = (max(0, -steps), min(count, count - steps))
    return lax.ppermute(value, axes, [(source, source + steps) for source in range(first, last)])


def exchange(value, axes):
    return lax.all_to_all(value, axes, split_axis=0, concat_axis=0, tiled=True)


def to_all(value, axes, count):
    rows, cols = value.shape
    copies = jnp.broadcast_to(value[None], (count, rows, cols)).reshape(count * rows, cols)
    return exchange(copies, axes)


def place_kernel(core_ref, part_ref, *refs):
    sp_ref, tm_ref, dn_ref, buf, sems = refs[-5:]
    lanes = pl.ds(pl.multiple_of(core_ref[0] * 128, 128), 128)
    copies = []
    for matrix in range(MATS):
        buf[matrix] = part_ref[pl.ds(matrix * C, C), :].astype(F32)
        if matrix < 18:
            target = sp_ref.at[matrix, :, lanes]
        elif matrix < 24:
            target = tm_ref.at[matrix - 18, :, lanes]
        else:
            target = dn_ref.at[matrix - 24, :, lanes]
        copies.append(pltpu.make_async_copy(buf.at[matrix], target, sems.at[matrix]))
        copies[-1].start()
    for copy in copies:
        copy.wait()


def place(which, part, outputs=()):
    whole = pl.BlockSpec(memory_space=pltpu.VMEM)
    hbm = pl.BlockSpec(memory_space=HBM)
    return pl.pallas_call(
        place_kernel,
        out_shape=(
            jax.ShapeDtypeStruct((18, C, C), F32),
            jax.ShapeDtypeStruct((6, C, C), F32),
            jax.ShapeDtypeStruct((3, C, C), F32),
        ),
        in_specs=[pl.BlockSpec(memory_space=pltpu.SMEM), whole] + [hbm] * len(outputs),
        out_specs=(hbm,) * 3,
        scratch_shapes=[pltpu.VMEM((MATS, C, 128), F32), pltpu.SemaphoreType.DMA((MATS,))],
        input_output_aliases={2 + i: i for i in range(len(outputs))},
        compiler_params=pltpu.CompilerParams(vmem_limit_bytes=16 * 1024 * 1024),
        cost_estimate=pl.CostEstimate(flops=0, bytes_accessed=6_000_000, transcendentals=0),
    )(which, part, *outputs)


def on_device(video, cotangent, gains, spatial_weights, time_weights, reduce_kernel_weights):
    tm = ("zh", "zl", "xl")
    video = video.reshape(FR * PIX, C)
    cot = cotangent.reshape(FR * 8, 4 * C)
    before = passed_along(video[-6 * PIX :], tm, 1)
    leading = [video[: 2 * PIX]] + [cot[:48, tap * C : (tap + 1) * C] for tap in range(4)]
    after = passed_along(jnp.concatenate(leading, axis=0), tm, -1)
    core = lax.axis_index("core").astype(jnp.int32).reshape(1)
    encoded, mine, theirs = run_model(
        core,
        video,
        before,
        after,
        cot,
        gains,
        spatial_weights.reshape(2, 9, C, C),
        time_weights,
        reduce_kernel_weights,
    )
    swap = [(0, 1), (1, 0)]
    other = lax.ppermute(theirs, "core", swap)
    half = (mine.astype(F32) + other.astype(F32)).astype(BF16)
    parts = exchange(half, PLANE).reshape(32, FLAT // 32, 128)
    part = jnp.sum(parts.astype(F32), axis=0).astype(BF16)
    parts = to_all(part, "zh", 4).reshape(4, FLAT // 32, 128)
    part = jnp.sum(parts.astype(F32), axis=0).astype(BF16)
    mine = to_all(part, PLANE, 32)
    other = lax.ppermute(mine, "core", swap)
    outputs = place(core, mine)
    grad_sp, grad_tm, grad_dn = place(1 - core, other, outputs)
    own_gn, other_gn = mine[ROWS : ROWS + 2].astype(F32), other[ROWS : ROWS + 2].astype(F32)
    grad_gn = jnp.concatenate(
        [jnp.where(core == 0, own_gn, other_gn), jnp.where(core == 0, other_gn, own_gn)], axis=1
    )
    return (
        encoded.reshape(1, FR // 2, 4, 4, 4 * C),
        grad_sp.reshape(2, 3, 3, C, C),
        grad_tm.reshape(2, 3, C, C),
        grad_dn,
        grad_gn,
    )


def solution(mesh):
    fine = Mesh(mesh.devices.reshape(2, 4, 2, 4, 2, 2), EVERY)
    split = P(("xh", "y", "core"), ("zh", "zl", "xl"), None, None, None)
    return jax.shard_map(
        on_device,
        mesh=fine,
        in_specs=(split, split, P(), P(), P(), P()),
        out_specs=(split, P(), P(), P(), P()),
        check_vma=False,
    )
```

```python
import jax
import jax.numpy as jnp
from jax import lax
from jax.experimental import pallas as pl
from jax.experimental.pallas import tpu as pltpu
from jax.sharding import Mesh, PartitionSpec as P

EPSILON = 1e-06
F32 = jnp.float32
BF16 = jnp.bfloat16
C = 256
PIX = 64
FR = 16
OUT = pltpu.VMEM
HBM = pltpu.HBM
MATS = 27
ROWS = MATS * C
CHUNK = 448
FLAT = 16 * CHUNK
EVERY = ("xh", "y", "core", "z", "xl")


def dot(left, right):
    return jnp.dot(left, right, preferred_element_type=F32)


def dot_nt(left, right):
    return lax.dot_general(left, right, (((1,), (1,)), ((), ())), preferred_element_type=F32)


def dot_tn(left, right):
    return lax.dot_general(left, right, (((0,), (0,)), ((), ())), preferred_element_type=F32)


def frames(first, count):
    return pl.ds(first * PIX, count * PIX)


def one_frame(index):
    return pl.ds(pl.multiple_of(index * PIX, PIX), PIX)


def write_windows(value, im_ref, rows, sign):
    grid = value.reshape(8, 8, C)
    column = lax.broadcasted_iota(jnp.int32, (8, 8, C), 1)
    blank = jnp.zeros((1, 8, C), F32)
    for j in range(3):
        dx = sign * (j - 1)
        if dx == 0:
            moved = grid
        elif dx == 1:
            moved = jnp.where(column == 7, 0.0, pltpu.roll(grid, 7, 1))
        else:
            moved = jnp.where(column == 0, 0.0, pltpu.roll(grid, 1, 1))
        for i in range(3):
            dy = sign * (i - 1)
            if dy == 0:
                placed = moved
            elif dy == 1:
                placed = jnp.concatenate([moved[1:], blank], axis=0)
            else:
                placed = jnp.concatenate([blank, moved[:-1]], axis=0)
            tap = 3 * i + j
            im_ref[rows, tap * C : (tap + 1) * C] = placed.reshape(PIX, C).astype(BF16)


def place_matrix(groups):
    size = groups * 8
    dest = lax.broadcasted_iota(jnp.int32, (size, size), 0)
    src = lax.broadcasted_iota(jnp.int32, (size, size), 1)
    want = (dest & 1) * (groups * 4) + (dest >> 3) * 4 + ((dest >> 1) & 3)
    return jnp.where(src == want, 1.0, 0.0).astype(BF16)


def ungroup(piece, groups, one_hot):
    halves = []
    for i in range(2):
        both = jnp.concatenate([piece(2 * i + j) for j in range(2)], axis=0)
        halves.append(dot(one_hot, both).reshape(groups, 8, C))
    return jnp.concatenate(halves, axis=1).reshape(groups * 16, C).astype(BF16)


def norm_only(src, first, count, gain, n_ref, to):
    for index in range(count):
        value = src[frames(first + index, 1), :].astype(F32)
        inv = lax.rsqrt(jnp.mean(value * value, axis=-1, keepdims=True) + EPSILON)
        n_ref[frames(to + index, 1), :] = (value * inv * gain).astype(BF16)


def norm_windows(src, first, count, gain, im, n_ref=None):
    def body(index, _):
        rows = one_frame(index)
        value = src[one_frame(index + first), :].astype(F32)
        inv = lax.rsqrt(jnp.mean(value * value, axis=-1, keepdims=True) + EPSILON)
        value = value * inv * gain
        write_windows(value, im, rows, 1)
        if n_ref is not None:
            n_ref[rows, :] = value.astype(BF16)
        return 0

    lax.fori_loop(0, count, body, 0, unroll=True)


def activate(im, weights, pieces, act, slope):
    for first, size, act_first, slope_first in pieces:
        conv = dot(im[pl.ds(first, size), :], weights.reshape(9 * C, C))
        logistic = jax.nn.sigmoid(conv)
        act[pl.ds(act_first, size), :] = (conv * logistic).astype(BF16)
        if slope_first is not None:
            slope_value = logistic * (1.0 + conv * (1.0 - logistic))
            slope[pl.ds(slope_first, size), :] = slope_value.astype(slope.dtype)


def side_by_side(raw_ref, count, flat_ref):
    for group in range(count):
        rows = raw_ref[group].astype(F32)
        for tap in range(4):
            first = tap * count * 4 + group * 4
            flat_ref[first : first + 4, :] = rows[:, tap * C : (tap + 1) * C]


def edge_kernel(video_hbm, cot_hbm, last_ref, first_ref, raw, flat, sems):
    copies = [
        pltpu.make_async_copy(cot_hbm.at[pl.ds(0, 12)], raw, sems.at[0]),
        pltpu.make_async_copy(video_hbm.at[frames(10, 6)], last_ref, sems.at[1]),
        pltpu.make_async_copy(video_hbm.at[frames(0, 2)], first_ref.at[frames(0, 2)], sems.at[2]),
    ]
    for copy in copies:
        copy.start()
    copies[0].wait()
    side_by_side(raw, 12, flat)
    first_ref[2 * PIX :, :] = flat[...].astype(BF16)
    copies[1].wait()
    copies[2].wait()


def edges(video, cot):
    whole = pl.BlockSpec(memory_space=pltpu.VMEM)
    hbm = pl.BlockSpec(memory_space=HBM)
    return pl.pallas_call(
        edge_kernel,
        out_shape=(OUT((6 * PIX, C), BF16), OUT((5 * PIX, C), BF16)),
        in_specs=[hbm, hbm],
        out_specs=(whole, whole),
        scratch_shapes=[
            pltpu.VMEM((12, 4, 4 * C), BF16),
            pltpu.VMEM((3 * PIX, C), F32),
            pltpu.SemaphoreType.DMA((3,)),
        ],
        compiler_params=pltpu.CompilerParams(vmem_limit_bytes=8 * 1024 * 1024),
        cost_estimate=pl.CostEstimate(flops=0, bytes_accessed=1_000_000, transcendentals=0),
    )(video, cot)


def with_edge(act, first, count):
    return jnp.concatenate([act[frames(first - k, count), :] for k in range(3)], axis=1)


def unpacked(pack_ref):
    return [pack_ref.at[frames(first, count)] for first, count in ((0, 16), (16, 14), (30, 14))]


def front_kernel(
    video_hbm,
    gains_hbm,
    sw_hbm,
    tw_hbm,
    pack_ref,
    slope1_ref,
    s2_ref,
    gains,
    sw_ref,
    tw_ref,
    im1,
    im2,
    video,
    sems,
):
    a1_ref, a2_ref, slope2_ref = unpacked(pack_ref)
    pairs = [
        (video_hbm, video),
        (gains_hbm, gains),
        (sw_hbm.at[0], sw_ref.at[0]),
        (tw_hbm, tw_ref),
        (sw_hbm.at[1], sw_ref.at[1]),
    ]
    copies = [pltpu.make_async_copy(*pair, sems.at[i]) for i, pair in enumerate(pairs)]
    for copy in copies:
        copy.start()
    copies[0].wait()
    copies[1].wait()
    norm_windows(video, 0, FR, gains[0:1, :], im1)
    for copy in copies[2:]:
        copy.wait()
    activate(im1, sw_ref[0], [(0, 512, 0, 0), (512, 512, 512, 512)], a1_ref, slope1_ref)
    later = with_edge(a1_ref, 2, 14)
    s2_ref[...] = video[frames(2, 14), :].astype(F32) + dot(later, tw_ref[0].reshape(3 * C, C))
    norm_windows(s2_ref, 0, 14, gains[1:2, :], im2)
    activate(im2, sw_ref[1], [(0, 448, 0, 0), (448, 448, 448, 448)], a2_ref, slope2_ref)


def model_kernel(
    core_ref,
    before_ref,
    after_ref,
    gains_hbm,
    sw_hbm,
    tw_hbm,
    rw_hbm,
    video_hbm,
    cot_hbm,
    pack_ref,
    slope1,
    s2_own,
    enc_ref,
    mine_ref,
    theirs_ref,
    s1,
    s2,
    im,
    n2_ref,
    a1,
    a2,
    slope2,
    low,
    cotf,
    up,
    g2,
    g1,
    ga,
    gn,
    wcat,
    gains_ref,
    sw_ref,
    tw_ref,
    rw_ref,
    s1_own,
    n1_ref,
    cot_raw,
    cot_flat,
    sems,
):
    pairs = [
        (gains_hbm, gains_ref),
        (sw_hbm.at[0], sw_ref.at[0]),
        (tw_hbm, tw_ref),
        (video_hbm, s1_own),
        (sw_hbm.at[1], sw_ref.at[1]),
        (rw_hbm, rw_ref),
        (cot_hbm, cot_raw),
    ]
    copies = [pltpu.make_async_copy(*pair, sems.at[i]) for i, pair in enumerate(pairs)]
    for copy in copies:
        copy.start()
    s1[frames(0, 6), :] = before_ref[...].astype(F32)
    s1[frames(22, 2), :] = after_ref[: 2 * PIX].astype(F32)
    a1_own, a2_own, slope2_own = unpacked(pack_ref)
    a1[frames(6, 16), :] = a1_own[...]
    s2[frames(5, 14), :] = s2_own[...]
    a2[frames(5, 14), :] = a2_own[...]
    slope2[frames(5, 14), :] = slope2_own[...].astype(F32)
    n_refs = (n1_ref, n2_ref)
    first_core = core_ref[0] == 0

    def put_halves(rows, value):
        low_half = value[:, :128].astype(BF16)
        high_half = value[:, 128:].astype(BF16)
        mine_ref[rows, :] = jnp.where(first_core, low_half, high_half)
        theirs_ref[rows, :] = jnp.where(first_core, high_half, low_half)

    def put(matrix, value):
        put_halves(pl.ds(matrix * C, C), value)

    copies[0].wait()
    norm_windows(s1, 0, 6, gains_ref[0:1, :], im)
    norm_windows(s1, 22, 2, gains_ref[0:1, :], im.at[frames(6, 2)])
    for copy in copies[1:]:
        copy.wait()
    activate(im, sw_ref[0], [(0, 384, 0, None), (384, 128, 1408, None)], a1, None)
    norm_only(s1_own, 0, FR, gains_ref[0:1, :], n1_ref, 0)
    norm_only(s2, 5, 14, gains_ref[1:2, :], n2_ref, 2)
    side_by_side(cot_raw, 32, cot_flat)
    ends = jnp.concatenate([with_edge(a1, 3, 5), with_edge(a1, 22, 2)], axis=0)
    ends = dot(ends, tw_ref[0].reshape(3 * C, C))
    s2[frames(0, 3), :] = s1[frames(3, 3), :] + ends[: 3 * PIX]
    s2[frames(3, 2), :] = s1_own[frames(0, 2), :].astype(F32) + ends[3 * PIX : 5 * PIX]
    s2[frames(19, 2), :] = s1[frames(22, 2), :] + ends[5 * PIX :]
    norm_windows(s2, 0, 3, gains_ref[1:2, :], im.at[frames(8, 3)])
    norm_windows(s2, 3, 2, gains_ref[1:2, :], im.at[frames(11, 2)], n2_ref)
    norm_windows(s2, 19, 2, gains_ref[1:2, :], im.at[frames(13, 2)])
    activate(im, sw_ref[1], [(512, 320, 0, 0), (832, 128, 1216, 1216)], a2, slope2)
    total = dot(with_edge(a2, 2, 17), tw_ref[1].reshape(3 * C, C))
    low[frames(0, 17), :] = (s2[frames(2, 17), :] + total).astype(BF16)
    low[frames(17, 1), :] = jnp.zeros((PIX, C), BF16)

    pairs = low[...].reshape(9, 2 * PIX, C)
    taps = jnp.concatenate(
        [
            pairs[1:9, :PIX].reshape(8 * PIX, C),
            pairs[0:8, PIX:].reshape(8 * PIX, C),
            pairs[0:8, :PIX].reshape(8 * PIX, C),
        ],
        axis=1,
    )
    one_hot = place_matrix(32)
    down = dot(taps, rw_ref[...].reshape(3 * C, C)).astype(BF16).astype(F32)
    down = down.reshape(32, 16, C)
    for i in range(2):
        both = dot_tn(one_hot, down[:, i * 8 : (i + 1) * 8].reshape(256, C).astype(BF16))
        for j in range(2):
            tap = 2 * i + j
            enc_ref[:, tap * C : (tap + 1) * C] = both[j * 128 : (j + 1) * 128].astype(BF16)
    cotf[frames(0, 8), :] = ungroup(
        lambda tap: cot_flat[tap * 128 : (tap + 1) * 128, :].astype(BF16), 32, one_hot
    )
    cotf[frames(8, 3), :] = ungroup(
        lambda tap: after_ref[2 * PIX + tap * 48 : 2 * PIX + (tap + 1) * 48, :],
        12,
        place_matrix(12),
    )
    grad_down = dot_tn(taps, cotf[frames(0, 8), :])
    for k in range(3):
        put(24 + k, grad_down[k * C : (k + 1) * C])
    even = dot_nt(cotf[frames(0, 10), :], rw_ref[1])
    odd = dot_nt(cotf[frames(0, 10), :], rw_ref[0]) + dot_nt(cotf[frames(1, 10), :], rw_ref[2])
    merged = jnp.concatenate(
        [even.reshape(10, PIX, C), odd.reshape(10, PIX, C)], axis=1
    ).reshape(20 * PIX, C)
    up[...] = merged[: 18 * PIX]
    g2[...] = merged.astype(BF16)

    def block_back(block, grad, act, own, slope, slope_own, count, pieces):
        grad_time = dot_tn(with_edge(act, own, FR), grad[frames(0, FR), :])
        for k in range(3):
            put(18 + 3 * block + k, grad_time[k * C : (k + 1) * C])
        for k in range(3):
            wcat[:, k * C : (k + 1) * C] = tw_ref[block, k]
        for first, size in pieces:
            later = jnp.concatenate(
                [grad[pl.ds(first + k * PIX, size), :] for k in range(3)], axis=1
            )
            ga[pl.ds(first, size), :] = dot_nt(later, wcat[:, : 3 * C])

        def body(index, _):
            rows = one_frame(index)
            write_windows(ga[rows, :] * slope[one_frame(index + slope_own), :].astype(F32), im, rows, -1)
            return 0

        lax.fori_loop(0, count, body, 0, unroll=True)
        for tap in range(9):
            wcat[:, tap * C : (tap + 1) * C] = sw_ref[block, tap]
        for first, size in pieces:
            gn[pl.ds(first, size), :] = dot_nt(im[pl.ds(first, size), :], wcat[...])
        grad_sp = dot_tn(n_refs[block][...], im[frames(0, FR), :])
        for tap in range(9):
            put(9 * block + tap, grad_sp[:, tap * C : (tap + 1) * C])

    def gain_part(index, src, own):
        value = src[one_frame(index + own), :].astype(F32)
        inv = lax.rsqrt(jnp.mean(value * value, axis=-1, keepdims=True) + EPSILON)
        unit = value * inv
        grad = gn[one_frame(index), :]
        return grad, unit, inv

    block_back(1, g2, a2, 3, slope2, 3, 18, [(0, 576), (576, 576)])
    gain = gains_ref[1:2, :]

    def norm_back(index, total):
        grad, unit, inv = gain_part(index, s2, 3)
        scaled = grad * gain
        back = inv * (scaled - unit * jnp.mean(unit * scaled, axis=-1, keepdims=True))
        rows = one_frame(index)
        g1[rows, :] = (up[rows, :] + back).astype(BF16)
        return total + jnp.sum((grad * unit).reshape(8, 8, C), axis=0)

    none = jnp.zeros((8, C), F32)
    total2 = lax.fori_loop(0, FR, norm_back, none, unroll=True)
    lax.fori_loop(FR, FR + 2, norm_back, none, unroll=True)

    block_back(0, g1, a1, 6, slope1, 0, 16, [(0, 512), (512, 512)])

    def gain_only(index, total):
        grad, unit, _ = gain_part(index, s1_own, 0)
        return total + jnp.sum((grad * unit).reshape(8, 8, C), axis=0)

    total1 = lax.fori_loop(0, FR, gain_only, none, unroll=True)
    rest = jnp.concatenate(
        [
            jnp.sum(total1, axis=0, keepdims=True),
            jnp.sum(total2, axis=0, keepdims=True),
            jnp.zeros((14, C), F32),
        ],
        axis=0,
    )
    put_halves(pl.ds(ROWS, 16), rest)
    for ref in (mine_ref, theirs_ref):
        ref[ROWS + 16 :, :] = jnp.zeros((FLAT - ROWS - 16, 128), BF16)


def run_model(core, video, before, after, cot, gains, sw, tw, rw):
    def vm(rows, dtype, cols=C):
        return pltpu.VMEM((rows * PIX, cols), dtype)

    whole = pl.BlockSpec(memory_space=pltpu.VMEM)
    hbm = pl.BlockSpec(memory_space=HBM)
    own = [(44, BF16), (16, F32), (14, F32)]
    known = pl.pallas_call(
        front_kernel,
        out_shape=tuple(OUT((count * PIX, C), dtype) for count, dtype in own),
        in_specs=[hbm] * 4,
        out_specs=(whole,) * 3,
        scratch_shapes=[
            pltpu.VMEM((2, C), F32),
            pltpu.VMEM((2, 9, C, C), BF16),
            pltpu.VMEM((2, 3, C, C), BF16),
            vm(16, BF16, 9 * C),
            vm(14, BF16, 9 * C),
            vm(16, BF16),
            pltpu.SemaphoreType.DMA((5,)),
        ],
        compiler_params=pltpu.CompilerParams(vmem_limit_bytes=24 * 1024 * 1024),
        cost_estimate=pl.CostEstimate(
            flops=3_500_000_000, bytes_accessed=4_000_000, transcendentals=500_000
        ),
    )(video, gains, sw, tw)
    return pl.pallas_call(
        model_kernel,
        out_shape=(
            jax.ShapeDtypeStruct((128, 4 * C), BF16),
            OUT((FLAT, 128), BF16),
            OUT((FLAT, 128), BF16),
        ),
        in_specs=[pl.BlockSpec(memory_space=pltpu.SMEM)] + [whole] * 2 + [hbm] * 6 + [whole] * 3,
        out_specs=(whole, whole, whole),
        scratch_shapes=[
            vm(24, F32),
            vm(21, F32),
            vm(18, BF16, 9 * C),
            vm(16, BF16),
            vm(24, BF16),
            vm(21, BF16),
            vm(21, F32),
            vm(18, BF16),
            vm(11, BF16),
            vm(18, F32),
            vm(20, BF16),
            vm(18, BF16),
            vm(18, F32),
            vm(18, F32),
            pltpu.VMEM((C, 9 * C), BF16),
            pltpu.VMEM((2, C), F32),
            pltpu.VMEM((2, 9, C, C), BF16),
            pltpu.VMEM((2, 3, C, C), BF16),
            pltpu.VMEM((3, C, C), BF16),
            vm(16, BF16),
            vm(16, BF16),
            pltpu.VMEM((32, 4, 4 * C), BF16),
            pltpu.VMEM((8 * PIX, C), F32),
            pltpu.SemaphoreType.DMA((7,)),
        ],
        compiler_params=pltpu.CompilerParams(vmem_limit_bytes=30 * 1024 * 1024),
        cost_estimate=pl.CostEstimate(
            flops=9_000_000_000, bytes_accessed=6_000_000, transcendentals=1_000_000
        ),
    )(core, before, after, gains, sw, tw, rw, video, cot, *known)


def passed_along(value, axes, steps):
    count = lax.axis_size(axes)
    first, last = (max(0, -steps), min(count, count - steps))
    return lax.ppermute(value, axes, [(source, source + steps) for source in range(first, last)])


def position(x, y, core, z):
    return ((x // 2 * 4 + y) * 2 + core) * 16 + z % 8 * 2 + x % 2


def wide_groups():
    groups = []
    for fixed in range(4):
        for pair in range(4):
            ends = (2 * pair, 2 * pair + 1)
            groups.append([position(x, fixed, 0, z) for x in range(4) for z in ends])
            ends = (2 * pair + 1, 2 * pair + 2)
            groups.append([position(fixed, y, 1, z) for y in range(4) for z in ends])
    return groups


def cross_groups():
    groups = []
    for fixed in range(4):
        for z in range(8):
            groups.append([position(fixed, y, 0, z) for y in range(4)])
            groups.append([position(x, fixed, 1, z) for x in range(4)])
    return groups


def rest_groups():
    return [
        [position(x, y, core, z) for z in range(parity, 8, 2)]
        for x in range(4)
        for y in range(4)
        for core in range(2)
        for parity in range(2)
    ]


def exchange(value, groups):
    return lax.all_to_all(
        value, EVERY, split_axis=0, concat_axis=0, tiled=True, axis_index_groups=groups
    )


def to_all(value, groups):
    rows, cols = value.shape
    count = len(groups[0])
    copies = jnp.broadcast_to(value[None], (count, rows, cols)).reshape(count * rows, cols)
    return exchange(copies, groups)


def sum_parts(parts, groups):
    count = len(groups[0])
    parts = parts.reshape(count, parts.shape[0] // count, parts.shape[1])
    return jnp.sum(parts.astype(F32), axis=0).astype(BF16)


def place_kernel(core_ref, part_ref, gains_ref, *refs):
    sp_ref, tm_ref, dn_ref, gn_ref, buf, small, sems = refs[-7:]
    lanes = pl.ds(pl.multiple_of(core_ref[0] * 128, 128), 128)
    ours = part_ref[ROWS : ROWS + 16, :].astype(F32)[:2]
    theirs = gains_ref[ROWS : ROWS + 16, :].astype(F32)[:2]
    first_core = core_ref[0] == 0
    small[:, :128] = jnp.where(first_core, ours, theirs)
    small[:, 128:] = jnp.where(first_core, theirs, ours)
    copies = [pltpu.make_async_copy(small, gn_ref, sems.at[0])]
    copies[0].start()
    for target, first, spans in ((sp_ref, 0, (3, 5, 5, 5)), (tm_ref, 18, (6,)), (dn_ref, 24, (3,))):
        start = first
        for span in spans:
            for matrix in range(start, start + span):
                buf[matrix] = part_ref[pl.ds(matrix * C, C), :].astype(F32)
            copy = pltpu.make_async_copy(
                buf.at[pl.ds(start, span)],
                target.at[pl.ds(start - first, span), :, lanes],
                sems.at[len(copies)],
            )
            copy.start()
            copies.append(copy)
            start += span
    for copy in copies:
        copy.wait()


def place(which, part, gains, outputs=()):
    whole = pl.BlockSpec(memory_space=pltpu.VMEM)
    hbm = pl.BlockSpec(memory_space=HBM)
    return pl.pallas_call(
        place_kernel,
        out_shape=(
            jax.ShapeDtypeStruct((18, C, C), F32),
            jax.ShapeDtypeStruct((6, C, C), F32),
            jax.ShapeDtypeStruct((3, C, C), F32),
            jax.ShapeDtypeStruct((2, C), F32),
        ),
        in_specs=[pl.BlockSpec(memory_space=pltpu.SMEM), whole, whole] + [hbm] * len(outputs),
        out_specs=(hbm,) * 4,
        scratch_shapes=[
            pltpu.VMEM((MATS, C, 128), F32),
            pltpu.VMEM((2, C), F32),
            pltpu.SemaphoreType.DMA((7,)),
        ],
        input_output_aliases={3 + i: i for i in range(len(outputs))},
        compiler_params=pltpu.CompilerParams(vmem_limit_bytes=16 * 1024 * 1024),
        cost_estimate=pl.CostEstimate(flops=0, bytes_accessed=6_000_000, transcendentals=0),
    )(which, part, gains, *outputs)


def on_device(video, cotangent, gains, spatial_weights, time_weights, reduce_kernel_weights):
    tm = ("z", "xl")
    video, cot, gains, sw, tw, rw = (
        pltpu.with_memory_space_constraint(value, HBM)
        for value in (
            video.reshape(FR * PIX, C),
            cotangent.reshape(FR * 2, 4, 4 * C),
            gains,
            spatial_weights.reshape(2, 9, C, C),
            time_weights,
            reduce_kernel_weights,
        )
    )
    last, first = edges(video, cot)
    before = passed_along(last, tm, 1)
    after = passed_along(first, tm, -1)
    core = lax.axis_index("core").astype(jnp.int32).reshape(1)
    encoded, mine, theirs = run_model(
        core,
        video,
        before,
        after,
        cot,
        gains,
        sw,
        tw,
        rw,
    )
    swap = [(0, 1), (1, 0)]
    other = lax.ppermute(theirs, "core", swap)
    half = (mine.astype(F32) + other.astype(F32)).astype(BF16)
    wide, cross, rest = wide_groups(), cross_groups(), rest_groups()
    part = sum_parts(exchange(half, wide), wide)
    part = sum_parts(exchange(part, cross), cross)
    part = sum_parts(to_all(part, rest), rest)
    mine = to_all(to_all(part, cross), wide)
    other = lax.ppermute(mine, "core", swap)
    outputs = place(core, mine, mine)[:3]
    grad_sp, grad_tm, grad_dn, grad_gn = place(1 - core, other, mine, outputs)
    return (
        encoded.reshape(1, FR // 2, 4, 4, 4 * C),
        grad_sp.reshape(2, 3, 3, C, C),
        grad_tm.reshape(2, 3, C, C),
        grad_dn,
        grad_gn,
    )


def solution(mesh):
    fine = Mesh(mesh.devices.reshape(2, 4, 2, 8, 2), EVERY)
    split = P(("xh", "y", "core"), ("z", "xl"), None, None, None)
    return jax.shard_map(
        on_device,
        mesh=fine,
        in_specs=(split, split, P(), P(), P(), P()),
        out_specs=(split, P(), P(), P(), P()),
        check_vma=False,
    )
```

```python
import jax
import jax.numpy as jnp
from jax import lax
from jax.experimental import pallas as pl
from jax.experimental.pallas import tpu as pltpu
from jax.sharding import Mesh, PartitionSpec as P

EPSILON = 1e-06
F32 = jnp.float32
BF16 = jnp.bfloat16
C = 256
PIX = 64
FR = 16
OUT = pltpu.VMEM
HBM = pltpu.HBM
MATS = 27
ROWS = MATS * C
CHUNK = 448
FLAT = 16 * CHUNK
EVERY = ("xh", "y", "core", "z", "xl")


def dot(left, right):
    return jnp.dot(left, right, preferred_element_type=F32)


def dot_nt(left, right):
    return lax.dot_general(left, right, (((1,), (1,)), ((), ())), preferred_element_type=F32)


def dot_tn(left, right):
    return lax.dot_general(left, right, (((0,), (0,)), ((), ())), preferred_element_type=F32)


def frames(first, count):
    return pl.ds(first * PIX, count * PIX)


def one_frame(index):
    return pl.ds(pl.multiple_of(index * PIX, PIX), PIX)


def write_windows(value, im_ref, rows, sign):
    grid = value.reshape(8, 8, C)
    column = lax.broadcasted_iota(jnp.int32, (8, 8, C), 1)
    blank = jnp.zeros((1, 8, C), F32)
    for j in range(3):
        dx = sign * (j - 1)
        if dx == 0:
            moved = grid
        elif dx == 1:
            moved = jnp.where(column == 7, 0.0, pltpu.roll(grid, 7, 1))
        else:
            moved = jnp.where(column == 0, 0.0, pltpu.roll(grid, 1, 1))
        for i in range(3):
            dy = sign * (i - 1)
            if dy == 0:
                placed = moved
            elif dy == 1:
                placed = jnp.concatenate([moved[1:], blank], axis=0)
            else:
                placed = jnp.concatenate([blank, moved[:-1]], axis=0)
            tap = 3 * i + j
            im_ref[rows, tap * C : (tap + 1) * C] = placed.reshape(PIX, C).astype(BF16)


def place_matrix(groups):
    size = groups * 8
    dest = lax.broadcasted_iota(jnp.int32, (size, size), 0)
    src = lax.broadcasted_iota(jnp.int32, (size, size), 1)
    want = (dest & 1) * (groups * 4) + (dest >> 3) * 4 + ((dest >> 1) & 3)
    return jnp.where(src == want, 1.0, 0.0).astype(BF16)


def ungroup(piece, groups, one_hot):
    halves = []
    for i in range(2):
        both = jnp.concatenate([piece(2 * i + j) for j in range(2)], axis=0)
        halves.append(dot(one_hot, both).reshape(groups, 8, C))
    return jnp.concatenate(halves, axis=1).reshape(groups * 16, C).astype(BF16)


def norm_only(src, first, count, gain, n_ref, to):
    for index in range(count):
        value = src[frames(first + index, 1), :].astype(F32)
        inv = lax.rsqrt(jnp.mean(value * value, axis=-1, keepdims=True) + EPSILON)
        n_ref[frames(to + index, 1), :] = (value * inv * gain).astype(BF16)


def norm_windows(src, first, count, gain, im, n_ref=None):
    def body(index, _):
        rows = one_frame(index)
        value = src[one_frame(index + first), :].astype(F32)
        inv = lax.rsqrt(jnp.mean(value * value, axis=-1, keepdims=True) + EPSILON)
        value = value * inv * gain
        write_windows(value, im, rows, 1)
        if n_ref is not None:
            n_ref[rows, :] = value.astype(BF16)
        return 0

    lax.fori_loop(0, count, body, 0, unroll=True)


def activate(im, weights, pieces, act, slope):
    for first, size, act_first, slope_first in pieces:
        conv = dot(im[pl.ds(first, size), :], weights.reshape(9 * C, C))
        logistic = jax.nn.sigmoid(conv)
        act[pl.ds(act_first, size), :] = (conv * logistic).astype(BF16)
        if slope_first is not None:
            slope_value = logistic * (1.0 + conv * (1.0 - logistic))
            slope[pl.ds(slope_first, size), :] = slope_value.astype(slope.dtype)


def side_by_side(raw_ref, count, flat_ref):
    for group in range(count):
        rows = raw_ref[group].astype(F32)
        for tap in range(4):
            first = tap * count * 4 + group * 4
            flat_ref[first : first + 4, :] = rows[:, tap * C : (tap + 1) * C]


def edge_kernel(video_hbm, cot_hbm, last_ref, first_ref, raw, flat, sems):
    copies = [
        pltpu.make_async_copy(cot_hbm.at[pl.ds(0, 12)], raw, sems.at[0]),
        pltpu.make_async_copy(video_hbm.at[frames(10, 6)], last_ref, sems.at[1]),
        pltpu.make_async_copy(video_hbm.at[frames(0, 2)], first_ref.at[frames(0, 2)], sems.at[2]),
    ]
    for copy in copies:
        copy.start()
    copies[0].wait()
    side_by_side(raw, 12, flat)
    first_ref[2 * PIX :, :] = flat[...].astype(BF16)
    copies[1].wait()
    copies[2].wait()


def edges(video, cot):
    whole = pl.BlockSpec(memory_space=pltpu.VMEM)
    hbm = pl.BlockSpec(memory_space=HBM)
    return pl.pallas_call(
        edge_kernel,
        out_shape=(OUT((6 * PIX, C), BF16), OUT((5 * PIX, C), BF16)),
        in_specs=[hbm, hbm],
        out_specs=(whole, whole),
        scratch_shapes=[
            pltpu.VMEM((12, 4, 4 * C), BF16),
            pltpu.VMEM((3 * PIX, C), F32),
            pltpu.SemaphoreType.DMA((3,)),
        ],
        compiler_params=pltpu.CompilerParams(vmem_limit_bytes=8 * 1024 * 1024),
        cost_estimate=pl.CostEstimate(flops=0, bytes_accessed=1_000_000, transcendentals=0),
    )(video, cot)


def with_edge(act, first, count):
    return jnp.concatenate([act[frames(first - k, count), :] for k in range(3)], axis=1)


def unpacked(pack_ref):
    return [pack_ref.at[frames(first, count)] for first, count in ((0, 16), (16, 14), (30, 14))]


def front_kernel(
    video_hbm,
    gains_hbm,
    sw_hbm,
    tw_hbm,
    pack_ref,
    slope1_ref,
    gains,
    sw_ref,
    tw_ref,
    s2_ref,
    im1,
    im2,
    video,
    sems,
):
    a1_ref, a2_ref, slope2_ref = unpacked(pack_ref)
    pairs = [
        (video_hbm, video),
        (gains_hbm, gains),
        (sw_hbm.at[0], sw_ref.at[0]),
        (tw_hbm, tw_ref),
        (sw_hbm.at[1], sw_ref.at[1]),
    ]
    copies = [pltpu.make_async_copy(*pair, sems.at[i]) for i, pair in enumerate(pairs)]
    for copy in copies:
        copy.start()
    copies[0].wait()
    copies[1].wait()
    norm_windows(video, 0, FR, gains[0:1, :], im1)
    for copy in copies[2:]:
        copy.wait()
    activate(im1, sw_ref[0], [(0, 512, 0, 0), (512, 512, 512, 512)], a1_ref, slope1_ref)
    later = with_edge(a1_ref, 2, 14)
    s2_ref[...] = video[frames(2, 14), :].astype(F32) + dot(later, tw_ref[0].reshape(3 * C, C))
    norm_windows(s2_ref, 0, 14, gains[1:2, :], im2)
    activate(im2, sw_ref[1], [(0, 448, 0, 0), (448, 448, 448, 448)], a2_ref, slope2_ref)


def model_kernel(
    core_ref,
    before_ref,
    after_ref,
    gains_hbm,
    sw_hbm,
    tw_hbm,
    rw_hbm,
    video_hbm,
    cot_hbm,
    pack_ref,
    slope1,
    enc_ref,
    mine_ref,
    theirs_ref,
    s1,
    s2,
    im,
    n2_ref,
    a1,
    a2,
    slope2,
    low,
    cotf,
    up,
    g2,
    g1,
    ga,
    gn,
    wcat,
    gains_ref,
    sw_ref,
    tw_ref,
    rw_ref,
    s1_own,
    n1_ref,
    cot_raw,
    cot_flat,
    sems,
):
    pairs = [
        (gains_hbm, gains_ref),
        (sw_hbm.at[0], sw_ref.at[0]),
        (tw_hbm, tw_ref),
        (video_hbm, s1_own),
        (sw_hbm.at[1], sw_ref.at[1]),
        (rw_hbm, rw_ref),
        (cot_hbm, cot_raw),
    ]
    copies = [pltpu.make_async_copy(*pair, sems.at[i]) for i, pair in enumerate(pairs)]
    for copy in copies:
        copy.start()
    s1[frames(0, 6), :] = before_ref[...].astype(F32)
    s1[frames(22, 2), :] = after_ref[: 2 * PIX].astype(F32)
    a1_own, a2_own, slope2_own = unpacked(pack_ref)
    a1[frames(6, 16), :] = a1_own[...]
    a2[frames(5, 14), :] = a2_own[...]
    slope2[frames(5, 14), :] = slope2_own[...].astype(F32)
    n_refs = (n1_ref, n2_ref)
    first_core = core_ref[0] == 0

    def put_halves(rows, value):
        low_half = value[:, :128].astype(BF16)
        high_half = value[:, 128:].astype(BF16)
        mine_ref[rows, :] = jnp.where(first_core, low_half, high_half)
        theirs_ref[rows, :] = jnp.where(first_core, high_half, low_half)

    def put(matrix, value):
        put_halves(pl.ds(matrix * C, C), value)

    copies[0].wait()
    norm_windows(s1, 0, 6, gains_ref[0:1, :], im)
    norm_windows(s1, 22, 2, gains_ref[0:1, :], im.at[frames(6, 2)])
    for copy in copies[1:]:
        copy.wait()
    activate(im, sw_ref[0], [(0, 384, 0, None), (384, 128, 1408, None)], a1, None)
    norm_only(s1_own, 0, FR, gains_ref[0:1, :], n1_ref, 0)
    middle = dot(with_edge(a1, 8, 14), tw_ref[0].reshape(3 * C, C))
    s2[frames(5, 14), :] = s1_own[frames(2, 14), :].astype(F32) + middle
    norm_only(s2, 5, 14, gains_ref[1:2, :], n2_ref, 2)
    side_by_side(cot_raw, 32, cot_flat)
    ends = jnp.concatenate([with_edge(a1, 3, 5), with_edge(a1, 22, 2)], axis=0)
    ends = dot(ends, tw_ref[0].reshape(3 * C, C))
    s2[frames(0, 3), :] = s1[frames(3, 3), :] + ends[: 3 * PIX]
    s2[frames(3, 2), :] = s1_own[frames(0, 2), :].astype(F32) + ends[3 * PIX : 5 * PIX]
    s2[frames(19, 2), :] = s1[frames(22, 2), :] + ends[5 * PIX :]
    norm_windows(s2, 0, 3, gains_ref[1:2, :], im.at[frames(8, 3)])
    norm_windows(s2, 3, 2, gains_ref[1:2, :], im.at[frames(11, 2)], n2_ref)
    norm_windows(s2, 19, 2, gains_ref[1:2, :], im.at[frames(13, 2)])
    activate(im, sw_ref[1], [(512, 320, 0, 0), (832, 128, 1216, 1216)], a2, slope2)
    total = dot(with_edge(a2, 2, 17), tw_ref[1].reshape(3 * C, C))
    low[frames(0, 17), :] = (s2[frames(2, 17), :] + total).astype(BF16)
    low[frames(17, 1), :] = jnp.zeros((PIX, C), BF16)

    pairs = low[...].reshape(9, 2 * PIX, C)
    taps = jnp.concatenate(
        [
            pairs[1:9, :PIX].reshape(8 * PIX, C),
            pairs[0:8, PIX:].reshape(8 * PIX, C),
            pairs[0:8, :PIX].reshape(8 * PIX, C),
        ],
        axis=1,
    )
    one_hot = place_matrix(32)
    down = dot(taps, rw_ref[...].reshape(3 * C, C)).astype(BF16).astype(F32)
    down = down.reshape(32, 16, C)
    for i in range(2):
        both = dot_tn(one_hot, down[:, i * 8 : (i + 1) * 8].reshape(256, C).astype(BF16))
        for j in range(2):
            tap = 2 * i + j
            enc_ref[:, tap * C : (tap + 1) * C] = both[j * 128 : (j + 1) * 128].astype(BF16)
    cotf[frames(0, 8), :] = ungroup(
        lambda tap: cot_flat[tap * 128 : (tap + 1) * 128, :].astype(BF16), 32, one_hot
    )
    cotf[frames(8, 3), :] = ungroup(
        lambda tap: after_ref[2 * PIX + tap * 48 : 2 * PIX + (tap + 1) * 48, :],
        12,
        place_matrix(12),
    )
    grad_down = dot_tn(taps, cotf[frames(0, 8), :])
    for k in range(3):
        put(24 + k, grad_down[k * C : (k + 1) * C])
    even = dot_nt(cotf[frames(0, 10), :], rw_ref[1])
    odd = dot_nt(cotf[frames(0, 10), :], rw_ref[0]) + dot_nt(cotf[frames(1, 10), :], rw_ref[2])
    merged = jnp.concatenate(
        [even.reshape(10, PIX, C), odd.reshape(10, PIX, C)], axis=1
    ).reshape(20 * PIX, C)
    up[...] = merged[: 18 * PIX]
    g2[...] = merged.astype(BF16)

    def block_back(block, grad, act, own, slope, slope_own, count, pieces):
        grad_time = dot_tn(with_edge(act, own, FR), grad[frames(0, FR), :])
        for k in range(3):
            put(18 + 3 * block + k, grad_time[k * C : (k + 1) * C])
        for k in range(3):
            wcat[:, k * C : (k + 1) * C] = tw_ref[block, k]
        for first, size in pieces:
            later = jnp.concatenate(
                [grad[pl.ds(first + k * PIX, size), :] for k in range(3)], axis=1
            )
            ga[pl.ds(first, size), :] = dot_nt(later, wcat[:, : 3 * C])

        def body(index, _):
            rows = one_frame(index)
            write_windows(ga[rows, :] * slope[one_frame(index + slope_own), :].astype(F32), im, rows, -1)
            return 0

        lax.fori_loop(0, count, body, 0, unroll=True)
        for tap in range(9):
            wcat[:, tap * C : (tap + 1) * C] = sw_ref[block, tap]
        for first, size in pieces:
            gn[pl.ds(first, size), :] = dot_nt(im[pl.ds(first, size), :], wcat[...])
        grad_sp = dot_tn(n_refs[block][...], im[frames(0, FR), :])
        for tap in range(9):
            put(9 * block + tap, grad_sp[:, tap * C : (tap + 1) * C])

    def gain_part(index, src, own):
        value = src[one_frame(index + own), :].astype(F32)
        inv = lax.rsqrt(jnp.mean(value * value, axis=-1, keepdims=True) + EPSILON)
        unit = value * inv
        grad = gn[one_frame(index), :]
        return grad, unit, inv

    block_back(1, g2, a2, 3, slope2, 3, 18, [(0, 576), (576, 576)])
    gain = gains_ref[1:2, :]

    def norm_back(index, total):
        grad, unit, inv = gain_part(index, s2, 3)
        scaled = grad * gain
        back = inv * (scaled - unit * jnp.mean(unit * scaled, axis=-1, keepdims=True))
        rows = one_frame(index)
        g1[rows, :] = (up[rows, :] + back).astype(BF16)
        return total + jnp.sum((grad * unit).reshape(8, 8, C), axis=0)

    none = jnp.zeros((8, C), F32)
    total2 = lax.fori_loop(0, FR, norm_back, none, unroll=True)
    lax.fori_loop(FR, FR + 2, norm_back, none, unroll=True)

    block_back(0, g1, a1, 6, slope1, 0, 16, [(0, 512), (512, 512)])

    def gain_only(index, total):
        grad, unit, _ = gain_part(index, s1_own, 0)
        return total + jnp.sum((grad * unit).reshape(8, 8, C), axis=0)

    total1 = lax.fori_loop(0, FR, gain_only, none, unroll=True)
    rest = jnp.concatenate(
        [
            jnp.sum(total1, axis=0, keepdims=True),
            jnp.sum(total2, axis=0, keepdims=True),
            jnp.zeros((14, C), F32),
        ],
        axis=0,
    )
    put_halves(pl.ds(ROWS, 16), rest)
    for ref in (mine_ref, theirs_ref):
        ref[ROWS + 16 :, :] = jnp.zeros((FLAT - ROWS - 16, 128), BF16)


def run_model(core, video, before, after, cot, gains, sw, tw, rw):
    def vm(rows, dtype, cols=C):
        return pltpu.VMEM((rows * PIX, cols), dtype)

    whole = pl.BlockSpec(memory_space=pltpu.VMEM)
    hbm = pl.BlockSpec(memory_space=HBM)
    own = [(44, BF16), (16, F32)]
    known = pl.pallas_call(
        front_kernel,
        out_shape=tuple(OUT((count * PIX, C), dtype) for count, dtype in own),
        in_specs=[hbm] * 4,
        out_specs=(whole,) * 2,
        scratch_shapes=[
            pltpu.VMEM((2, C), F32),
            pltpu.VMEM((2, 9, C, C), BF16),
            pltpu.VMEM((2, 3, C, C), BF16),
            vm(14, F32),
            vm(16, BF16, 9 * C),
            vm(14, BF16, 9 * C),
            vm(16, BF16),
            pltpu.SemaphoreType.DMA((5,)),
        ],
        compiler_params=pltpu.CompilerParams(vmem_limit_bytes=24 * 1024 * 1024),
        cost_estimate=pl.CostEstimate(
            flops=3_500_000_000, bytes_accessed=4_000_000, transcendentals=500_000
        ),
    )(video, gains, sw, tw)
    return pl.pallas_call(
        model_kernel,
        out_shape=(
            jax.ShapeDtypeStruct((128, 4 * C), BF16),
            OUT((FLAT, 128), BF16),
            OUT((FLAT, 128), BF16),
        ),
        in_specs=[pl.BlockSpec(memory_space=pltpu.SMEM)] + [whole] * 2 + [hbm] * 6 + [whole] * 2,
        out_specs=(whole, whole, whole),
        scratch_shapes=[
            vm(24, F32),
            vm(21, F32),
            vm(18, BF16, 9 * C),
            vm(16, BF16),
            vm(24, BF16),
            vm(21, BF16),
            vm(21, F32),
            vm(18, BF16),
            vm(11, BF16),
            vm(18, F32),
            vm(20, BF16),
            vm(18, BF16),
            vm(18, F32),
            vm(18, F32),
            pltpu.VMEM((C, 9 * C), BF16),
            pltpu.VMEM((2, C), F32),
            pltpu.VMEM((2, 9, C, C), BF16),
            pltpu.VMEM((2, 3, C, C), BF16),
            pltpu.VMEM((3, C, C), BF16),
            vm(16, BF16),
            vm(16, BF16),
            pltpu.VMEM((32, 4, 4 * C), BF16),
            pltpu.VMEM((8 * PIX, C), F32),
            pltpu.SemaphoreType.DMA((7,)),
        ],
        compiler_params=pltpu.CompilerParams(vmem_limit_bytes=30 * 1024 * 1024),
        cost_estimate=pl.CostEstimate(
            flops=9_000_000_000, bytes_accessed=6_000_000, transcendentals=1_000_000
        ),
    )(core, before, after, gains, sw, tw, rw, video, cot, *known)


def passed_along(value, axes, steps):
    count = lax.axis_size(axes)
    first, last = (max(0, -steps), min(count, count - steps))
    return lax.ppermute(value, axes, [(source, source + steps) for source in range(first, last)])


def position(x, y, core, z):
    return ((x // 2 * 4 + y) * 2 + core) * 16 + z % 8 * 2 + x % 2


def wide_groups():
    groups = []
    for fixed in range(4):
        for pair in range(4):
            ends = (2 * pair, 2 * pair + 1)
            groups.append([position(x, fixed, 0, z) for x in range(4) for z in ends])
            ends = (2 * pair + 1, 2 * pair + 2)
            groups.append([position(fixed, y, 1, z) for y in range(4) for z in ends])
    return groups


def cross_groups():
    groups = []
    for fixed in range(4):
        for z in range(8):
            groups.append([position(fixed, y, 0, z) for y in range(4)])
            groups.append([position(x, fixed, 1, z) for x in range(4)])
    return groups


def rest_groups():
    return [
        [position(x, y, core, z) for z in range(parity, 8, 2)]
        for x in range(4)
        for y in range(4)
        for core in range(2)
        for parity in range(2)
    ]


def exchange(value, groups):
    return lax.all_to_all(
        value, EVERY, split_axis=0, concat_axis=0, tiled=True, axis_index_groups=groups
    )


def to_all(value, groups):
    rows, cols = value.shape
    count = len(groups[0])
    copies = jnp.broadcast_to(value[None], (count, rows, cols)).reshape(count * rows, cols)
    return exchange(copies, groups)


def sum_parts(parts, groups):
    count = len(groups[0])
    parts = parts.reshape(count, parts.shape[0] // count, parts.shape[1])
    return jnp.sum(parts.astype(F32), axis=0).astype(BF16)


def place_kernel(core_ref, part_ref, gains_ref, *refs):
    sp_ref, tm_ref, dn_ref, gn_ref, buf, small, sems = refs[-7:]
    lanes = pl.ds(pl.multiple_of(core_ref[0] * 128, 128), 128)
    ours = part_ref[ROWS : ROWS + 16, :].astype(F32)[:2]
    theirs = gains_ref[ROWS : ROWS + 16, :].astype(F32)[:2]
    first_core = core_ref[0] == 0
    small[:, :128] = jnp.where(first_core, ours, theirs)
    small[:, 128:] = jnp.where(first_core, theirs, ours)
    copies = [pltpu.make_async_copy(small, gn_ref, sems.at[0])]
    copies[0].start()
    for target, first, spans in ((sp_ref, 0, (3, 5, 5, 5)), (tm_ref, 18, (6,)), (dn_ref, 24, (3,))):
        start = first
        for span in spans:
            for matrix in range(start, start + span):
                buf[matrix] = part_ref[pl.ds(matrix * C, C), :].astype(F32)
            copy = pltpu.make_async_copy(
                buf.at[pl.ds(start, span)],
                target.at[pl.ds(start - first, span), :, lanes],
                sems.at[len(copies)],
            )
            copy.start()
            copies.append(copy)
            start += span
    for copy in copies:
        copy.wait()


def place(which, part, gains, outputs=()):
    whole = pl.BlockSpec(memory_space=pltpu.VMEM)
    hbm = pl.BlockSpec(memory_space=HBM)
    return pl.pallas_call(
        place_kernel,
        out_shape=(
            jax.ShapeDtypeStruct((18, C, C), F32),
            jax.ShapeDtypeStruct((6, C, C), F32),
            jax.ShapeDtypeStruct((3, C, C), F32),
            jax.ShapeDtypeStruct((2, C), F32),
        ),
        in_specs=[pl.BlockSpec(memory_space=pltpu.SMEM), whole, whole] + [hbm] * len(outputs),
        out_specs=(hbm,) * 4,
        scratch_shapes=[
            pltpu.VMEM((MATS, C, 128), F32),
            pltpu.VMEM((2, C), F32),
            pltpu.SemaphoreType.DMA((7,)),
        ],
        input_output_aliases={3 + i: i for i in range(len(outputs))},
        compiler_params=pltpu.CompilerParams(vmem_limit_bytes=16 * 1024 * 1024),
        cost_estimate=pl.CostEstimate(flops=0, bytes_accessed=6_000_000, transcendentals=0),
    )(which, part, gains, *outputs)


def on_device(video, cotangent, gains, spatial_weights, time_weights, reduce_kernel_weights):
    tm = ("z", "xl")
    video, cot, gains, sw, tw, rw = (
        pltpu.with_memory_space_constraint(value, HBM)
        for value in (
            video.reshape(FR * PIX, C),
            cotangent.reshape(FR * 2, 4, 4 * C),
            gains,
            spatial_weights.reshape(2, 9, C, C),
            time_weights,
            reduce_kernel_weights,
        )
    )
    last, first = edges(video, cot)
    before = passed_along(last, tm, 1)
    after = passed_along(first, tm, -1)
    core = lax.axis_index("core").astype(jnp.int32).reshape(1)
    encoded, mine, theirs = run_model(
        core,
        video,
        before,
        after,
        cot,
        gains,
        sw,
        tw,
        rw,
    )
    swap = [(0, 1), (1, 0)]
    other = lax.ppermute(theirs, "core", swap)
    half = (mine.astype(F32) + other.astype(F32)).astype(BF16)
    wide, cross, rest = wide_groups(), cross_groups(), rest_groups()
    part = sum_parts(exchange(half, wide), wide)
    part = sum_parts(exchange(part, cross), cross)
    part = sum_parts(to_all(part, rest), rest)
    mine = to_all(to_all(part, cross), wide)
    other = lax.ppermute(mine, "core", swap)
    outputs = place(core, mine, mine)[:3]
    grad_sp, grad_tm, grad_dn, grad_gn = place(1 - core, other, mine, outputs)
    return (
        encoded.reshape(1, FR // 2, 4, 4, 4 * C),
        grad_sp.reshape(2, 3, 3, C, C),
        grad_tm.reshape(2, 3, C, C),
        grad_dn,
        grad_gn,
    )


def solution(mesh):
    fine = Mesh(mesh.devices.reshape(2, 4, 2, 8, 2), EVERY)
    split = P(("xh", "y", "core"), ("z", "xl"), None, None, None)
    return jax.shard_map(
        on_device,
        mesh=fine,
        in_specs=(split, split, P(), P(), P(), P()),
        out_specs=(split, P(), P(), P(), P()),
        check_vma=False,
    )
```
